32 devices in a mesh: nodes: 8 (over z, x), cols: 4 (over y, core).
Axes of the slice: x: 2, y: 2, z: 4, core: 2. Of those that a mesh axis runs over, the one named last changes fastest.
Arguments:
- node_feats: bfloat16 [8192, 256], P(('nodes', 'cols')), may hold values from -6 to 6
- tile_row: int32 [8, 1408], P('nodes', 'cols'), may hold values from 0 to 7, as said below
- tile_col: int32 [8, 1408], P('nodes', 'cols'), may hold values from 0 to 15
- tile_bits: int32 [8, 1408, 16, 128], P('nodes', 'cols'), may hold values from 0 to 255, as said below
- w_self: bfloat16 [256, 256], replicated, may hold values from -0.375 to 0.375
- w_neigh: bfloat16 [256, 256], replicated, may hold values from -1.5 to 1.5
- bias: float32 [256], replicated, may hold values from -3 to 3
- cotangent: bfloat16 [8192, 256], P(('nodes', 'cols')), may hold values from -6 to 6
Outputs:
- layer_out: bfloat16 [8192, 256], P(('nodes', 'cols'))
- feat_grad: bfloat16 [8192, 256], P(('nodes', 'cols'))
- self_grad: float32 [256, 256], replicated
- neigh_grad: float32 [256, 256], replicated
- bias_grad: float32 [256], replicated
The draws below stay inside these ranges and needn't reach their ends.
Inputs may be any that keep to these rules, and one draw needn't show every extreme that they name: `tile_row`: destination row block of a tile within its nodes group; in every nodes group at least one block carries no tile. `tile_col`: source row block of a tile within its cols index; a block may carry several tiles. `tile_bits`: bit j of word (w, a) of a tile is its edge from destination row a to source column 8 w + j; bits above the eighth are zero; some destination rows have no edge in any tile.
All inputs are finite; a program needn't handle non-finite values.
Results may differ from the reference program's by a relative error of at most 0.0075.
Values may be sent and summed in bfloat16 or wider, within the bound.
A program may use at most 64 MiB of HBM per device.

```python
import jax
import jax.numpy as jnp
from jax import lax

F = 256
H = 256
SPARSITY = 512
ROWS_DEV = 256
TILE_DEV = 352
NODES = 8192
TILES = 1408
DEST_BLOCKS = 8
SRC_BLOCKS = 16
N_NODES = 8
N_COLS = 4


def permute_blocks(group_key):
    return jax.random.permutation(group_key, DEST_BLOCKS)


def tile_layout(key):
    live_blocks = DEST_BLOCKS - max(1, DEST_BLOCKS // 8)
    first_rank = jax.random.randint(jax.random.fold_in(key, 101), (N_NODES, TILES), 0, live_blocks)
    second_rank = jax.random.randint(jax.random.fold_in(key, 102), (N_NODES, TILES), 0, live_blocks)
    block_rank = jnp.minimum(first_rank, second_rank).astype(jnp.int32)
    group_keys = jax.random.split(jax.random.fold_in(key, 103), N_NODES)
    labels = jax.vmap(permute_blocks)(group_keys).astype(jnp.int32)
    tile_row = jnp.take_along_axis(labels, block_rank, axis=1).astype(jnp.int32)
    isolated = (jax.random.randint(jax.random.fold_in(key, 104), (N_NODES, DEST_BLOCKS, 128), 0, 20) == 0).astype(jnp.int32)
    return (tile_row, isolated)


def draw_tile_row(key, part):
    return tile_layout(key)[0]


def draw_tile_bits(key, part):
    tile_row, isolated = tile_layout(key)
    group_index = jnp.arange(N_NODES, dtype=jnp.int32)[:, None]
    keep_rows = 1 - isolated[group_index, tile_row]
    packed = jnp.zeros((N_NODES, TILES, 16, 128), jnp.int32)
    for bit_index in range(8):
        edge_flags = (jax.random.randint(jax.random.fold_in(key, 200 + bit_index), (N_NODES, TILES, 16, 128), 0, SPARSITY) == 0).astype(jnp.int32)
        packed = packed + edge_flags * keep_rows[:, :, None, :] * 2 ** bit_index
    first_kept = jnp.argmax(keep_rows[:, 0, :], axis=1).astype(jnp.int32)
    row_ids = jnp.arange(128, dtype=jnp.int32)[None, :]
    dense_word = (row_ids == first_kept[:, None]) & (keep_rows[:, 0, :] == 1)
    packed = packed.at[:, 0, 0, :].set(jnp.where(dense_word, 255, packed[:, 0, 0, :]).astype(jnp.int32))
    return packed.astype(jnp.int32)


def touch_ends(entries, stream_key, smallest, largest):
    dims = entries.shape
    index_at = [jax.random.randint(jax.random.fold_in(stream_key, axis), (), 0, dims[axis]) for axis in range(len(dims))]
    entries = entries.at[tuple(index_at)].set(smallest)
    longest = dims.index(max(dims))
    index_at[longest] = (index_at[longest] + 1) % dims[longest]
    return entries.at[tuple(index_at)].set(largest)


def level_of(own_key, extent, cuts, least, high):
    level, own = 1.0, jax.random.fold_in(own_key, 6)
    for position, blocks in cuts:
        draws = jnp.exp(jax.random.uniform(jax.random.fold_in(own, position), (blocks,), jnp.float32, least / len(cuts), high / len(cuts)))
        level = level * jnp.repeat(draws, extent[position] // blocks).reshape([-1 if axis == position else 1 for axis in range(len(extent))])
    return level


def noise(own_key, shape, scale, reach, shards=(), kind=jnp.bfloat16):
    gain = level_of(own_key, shape, shards, -0.22, 0.18) if shards else 1.0
    array = jax.random.normal(own_key, shape, jnp.float32) * scale * gain
    return jnp.minimum(jnp.maximum(array, -reach), reach).astype(kind)


def setup_inputs(seed: int = 0) -> dict:
    arg_keys = jax.random.split(jax.random.key(seed), 9)
    node_feats = noise(arg_keys[0], (NODES, F), 1.0, 6.0, ((0, 32),))
    tile_row = draw_tile_row(jax.random.fold_in(arg_keys[8], 71), 0)
    tile_col = touch_ends(jax.random.randint(arg_keys[2], (N_NODES, TILES), 0, SRC_BLOCKS), jax.random.fold_in(arg_keys[2], 1), 0, SRC_BLOCKS - 1).astype(jnp.int32)
    tile_bits = draw_tile_bits(jax.random.fold_in(arg_keys[8], 71), 0)
    w_self = noise(arg_keys[4], (F, H), F ** -0.5, 0.375)
    w_neigh = noise(arg_keys[5], (F, H), (F // 16) ** -0.5, 1.5)
    bias = noise(arg_keys[6], (H,), 0.5, 3.0, (), jnp.float32)
    cotangent = noise(arg_keys[7], (NODES, H), 1.0, 6.0, ((0, 32),))
    return {"node_feats": node_feats, "tile_row": tile_row, "tile_col": tile_col, "tile_bits": tile_bits, "w_self": w_self, "w_neigh": w_neigh, "bias": bias, "cotangent": cotangent}


def unpack_tiles(packed):
    shifts = jnp.arange(8, dtype=jnp.int32)
    edge_flags = jnp.right_shift(packed[:, :, None, :], shifts[None, None, :, None]) & 1
    return edge_flags.reshape(packed.shape[0], 128, 128)


def reference(node_feats, tile_row, tile_col, tile_bits, w_self, w_neigh, bias, cotangent):
    per_dev = ROWS_DEV // 128
    total_blocks = NODES // 128
    feat_blocks = node_feats.reshape(total_blocks, 128, F)

    def tile_ids(device):
        node_idx = device // N_COLS
        col_idx = device % N_COLS
        first_tile = (col_idx * TILE_DEV).astype(jnp.int32)
        rows_here = lax.dynamic_slice_in_dim(tile_row[node_idx], first_tile, TILE_DEV, 0)
        cols_here = lax.dynamic_slice_in_dim(tile_col[node_idx], first_tile, TILE_DEV, 0)
        packed_here = lax.dynamic_slice_in_dim(tile_bits[node_idx], first_tile, TILE_DEV, 0)
        bits_here = unpack_tiles(packed_here).astype(jnp.float32)
        dest_block = (node_idx * DEST_BLOCKS + rows_here).astype(jnp.int32)
        source_block = (((cols_here // per_dev) * N_COLS + col_idx) * per_dev + cols_here % per_dev).astype(jnp.int32)
        return dest_block, source_block, bits_here

    def forward_step(totals, device):
        summed, degree = totals
        dest_block, source_block, bits_here = tile_ids(device)
        picked = feat_blocks[source_block].astype(jnp.float32)
        products = jnp.einsum('tba,tbf->taf', bits_here, picked)
        summed = summed.at[dest_block].add(products)
        degree = degree.at[dest_block].add(jnp.sum(bits_here, axis=1))
        return (summed, degree), None

    devices = jnp.arange(N_NODES * N_COLS, dtype=jnp.int32)
    initial = (jnp.zeros((total_blocks, 128, F), jnp.float32), jnp.zeros((total_blocks, 128), jnp.float32))
    (summed, degree), _ = lax.scan(forward_step, initial, devices)
    degree = jnp.maximum(degree.reshape(NODES), 1.0)
    neigh_mean = (summed.reshape(NODES, F) / degree[:, None]).astype(jnp.bfloat16)
    preact = jnp.dot(node_feats, w_self, preferred_element_type=jnp.float32) + jnp.dot(neigh_mean, w_neigh, preferred_element_type=jnp.float32) + bias
    sigmoid_pre = jax.nn.sigmoid(preact)
    layer_out = (preact * sigmoid_pre).astype(jnp.bfloat16)
    pre_grad = (cotangent.astype(jnp.float32) * sigmoid_pre * (1.0 + preact * (1.0 - sigmoid_pre))).astype(jnp.bfloat16)
    self_grad = jnp.dot(node_feats.T, pre_grad, preferred_element_type=jnp.float32)
    neigh_grad = jnp.dot(neigh_mean.T, pre_grad, preferred_element_type=jnp.float32)
    bias_grad = jnp.sum(pre_grad.astype(jnp.float32), axis=0)
    mean_grad = (jnp.dot(pre_grad, w_neigh.T, preferred_element_type=jnp.float32) / degree[:, None]).astype(jnp.bfloat16)
    grad_blocks = mean_grad.reshape(total_blocks, 128, F)

    def backward_step(src_grad, device):
        dest_block, source_block, bits_here = tile_ids(device)
        picked = grad_blocks[dest_block].astype(jnp.float32)
        products = jnp.einsum('tba,taf->tbf', bits_here, picked)
        return src_grad.at[source_block].add(products), None

    src_grad, _ = lax.scan(backward_step, jnp.zeros((total_blocks, 128, F), jnp.float32), devices)
    feat_grad = (jnp.dot(pre_grad, w_self.T, preferred_element_type=jnp.float32) + src_grad.reshape(NODES, F)).astype(jnp.bfloat16)
    return (layer_out, feat_grad, self_grad, neigh_grad, bias_grad)
```

```python
import functools

import jax
import jax.numpy as jnp
from jax import lax
from jax.experimental import pallas as pl
from jax.experimental.pallas import tpu as pltpu
from jax.sharding import PartitionSpec as P


def build_kernel(row_ref, col_ref, bits_ref, adj_ref, deg_ref, count_ref):
    source_count, dest_count = count_ref.shape[:2]
    tile_count = bits_ref.shape[0]
    zero = jnp.zeros((4, 16, 128), jnp.int32)

    def clear(s, _):
        for d in range(dest_count):
            count_ref[s, d] = zero
        return 0

    lax.fori_loop(0, source_count, clear, 0)

    def add_tile(t, _):
        r = row_ref[t]
        c = col_ref[t]
        word = bits_ref[t]
        spread = word | (word << 12)
        for j in range(4):
            count_ref[c, r, j] += (spread >> j) & 0x10001
        return 0

    lax.fori_loop(0, tile_count, add_tile, 0, unroll=4)

    deg_ref[...] = jnp.zeros_like(deg_ref)

    def expand(s, _):
        for d in range(dest_count):
            lanes = slice(d * 128, (d + 1) * 128)
            total = jnp.zeros((16, 128), jnp.float32)
            for j in range(4):
                pair = count_ref[s, d, j]
                low = (pair & 0xFFFF).astype(jnp.float32)
                high = (pair >> 16).astype(jnp.float32)
                total = total + (low + high)
                adj_ref[pl.ds(s * 128 + j * 16, 16), lanes] = low.astype(jnp.bfloat16)
                adj_ref[pl.ds(s * 128 + (j + 4) * 16, 16), lanes] = high.astype(jnp.bfloat16)
            deg_ref[:, lanes] += total
        return 0

    lax.fori_loop(0, source_count, expand, 0)


def build(tile_row, tile_col, tile_bits, source_count, dest_count):
    smem = pl.BlockSpec(memory_space=pltpu.SMEM)
    vmem = pl.BlockSpec(memory_space=pltpu.VMEM)
    return pl.pallas_call(
        build_kernel,
        out_shape=(
            jax.ShapeDtypeStruct((source_count * 128, dest_count * 128), jnp.bfloat16),
            jax.ShapeDtypeStruct((16, dest_count * 128), jnp.float32),
        ),
        in_specs=[smem, smem, vmem],
        out_specs=(vmem, vmem),
        scratch_shapes=[pltpu.VMEM((source_count, dest_count, 4, 16, 128), jnp.int32)],
        compiler_params=pltpu.CompilerParams(vmem_limit_bytes=48 * 1024 * 1024),
        cost_estimate=pl.CostEstimate(flops=20_000_000, bytes_accessed=8_000_000, transcendentals=0),
        name="build_adjacency",
    )(tile_row, tile_col, tile_bits)


def transposed(block):
    return block.astype(jnp.float32).T.astype(block.dtype)


def dot(left, right):
    return jnp.dot(left, right, preferred_element_type=jnp.float32)


def dot_nt(left, right):
    return lax.dot_general(left, right, (((1,), (1,)), ((), ())), preferred_element_type=jnp.float32)


def layer_kernel(node_count, col_count, piece, *refs):
    sources = refs[:node_count]
    (adj, deg, feats, w_self, w_neigh, bias, cot) = refs[node_count : node_count + 7]
    (layer_out, feat_grad, self_grad, neigh_grad, bias_grad) = refs[node_count + 7 : node_count + 12]
    (sum_out, sum_in, mean_all, src_out, src_in, part_out, part_in, node_out, node_in, full, sum_send, sum_recv, mean_send, mean_recv, src_send, src_recv, part_send, part_recv,
     node_send, node_recv, piece_send, piece_recv, full_send, full_recv) = refs[node_count + 12 :]
    n = lax.axis_index("nodes")
    c = lax.axis_index("cols")
    rows = feats.shape[0]
    width = feats.shape[1]
    f32, bf16 = jnp.float32, jnp.bfloat16

    def node_at(i):
        return lax.rem(n + i, node_count)

    def col_at(i):
        return lax.rem(c + i, col_count)

    def block(k):
        return pl.ds(pl.multiple_of(k * rows, rows), rows)

    def to_col(src, dst, send, recv, i):
        return pltpu.make_async_remote_copy(
            src_ref=src, dst_ref=dst, send_sem=send, recv_sem=recv,
            device_id=(n, col_at(i)), device_id_type=pl.DeviceIdType.MESH)

    def to_node(src, dst, send, recv, i):
        return pltpu.make_async_remote_copy(
            src_ref=src, dst_ref=dst, send_sem=send, recv_sem=recv,
            device_id=(node_at(i), c), device_id_type=pl.DeviceIdType.MESH)

    barrier = pltpu.get_barrier_semaphore()
    for i in range(1, col_count):
        pl.semaphore_signal(barrier, inc=1, device_id=(n, col_at(i)), device_id_type=pl.DeviceIdType.MESH)
    for i in range(1, node_count):
        pl.semaphore_signal(barrier, inc=1, device_id=(node_at(i), c), device_id_type=pl.DeviceIdType.MESH)
    pl.semaphore_wait(barrier, col_count + node_count - 2)

    def part_sum(col):
        total = jnp.zeros((width, rows), f32)
        for k in range(node_count):
            total = total + dot(sources[k][...], adj[block(lax.rem(n + node_count - k, node_count)), block(col)])
        return total

    def part_degree(col):
        return jnp.sum(deg[:, block(col)], axis=0, keepdims=True)

    def sum_copy(i):
        return to_col(sum_out.at[i - 1], sum_in.at[i - 1], sum_send.at[i - 1], sum_recv.at[i - 1], i)

    first = lax.broadcasted_iota(jnp.int32, (16, rows), 0) == 0

    def send_sum(i, _):
        col = col_at(i)
        sum_out[i - 1, :width] = part_sum(col).astype(bf16)
        degree = part_degree(col)
        high = jnp.floor(degree * (1.0 / 256.0))
        low = degree - high * 256.0
        sum_out[i - 1, width:] = jnp.where(first, high, low).astype(bf16)
        sum_copy(i).start()
        return 0

    lax.fori_loop(1, col_count, send_sum, 0)
    summed = part_sum(c)
    degree = part_degree(c)
    self_act = dot(feats[...], w_self[...]) + bias[...]
    feats_t = transposed(feats[...])
    for i in range(1, col_count):
        sum_copy(i).wait_recv()
        summed = summed + sum_in[i - 1, :width].astype(f32)
        tail = sum_in[i - 1, width:].astype(f32)
        degree = degree + tail[0:1] * 256.0 + tail[1:2]
    degree = jnp.maximum(degree, 1.0)

    mean_t = summed / degree
    mean = mean_t.T.astype(bf16)
    mean_t = mean_t.astype(bf16)
    preact = self_act + dot(mean, w_neigh[...])
    gate = jax.nn.sigmoid(preact)
    layer_out[...] = (preact * gate).astype(bf16)
    pre_grad = (cot[...].astype(f32) * gate * (1.0 + preact * (1.0 - gate))).astype(bf16)
    mean_grad = dot_nt(w_neigh[...], pre_grad) / degree
    mean_all[c] = mean_grad.T.astype(bf16)

    def mean_copy(i):
        return to_col(mean_all.at[c], mean_all.at[c], mean_send.at[i - 1], mean_recv.at[i - 1], i)

    for i in range(1, col_count):
        mean_copy(i).start()

    self_term = dot(feats_t, pre_grad)
    neigh_term = dot(mean_t, pre_grad)
    bias_term = jnp.sum(pre_grad.astype(f32), axis=0, keepdims=True)
    chunk = node_count * piece
    top = lax.broadcasted_iota(jnp.int32, (16, width), 0) == 0

    def split_bias(value):
        high = value.astype(bf16).astype(f32)
        return jnp.where(top, high, value - high).astype(bf16)

    def join_bias(value):
        pair = value.astype(f32)
        return pair[0:1] + pair[1:2]

    terms = jnp.concatenate([self_term, neigh_term], axis=0)
    spare = col_count * chunk - 2 * width
    if spare:
        terms = jnp.concatenate([terms, jnp.zeros((spare, width), f32)], axis=0)
    for k in range(col_count):
        part_out[k, :chunk] = terms[k * chunk : (k + 1) * chunk].astype(bf16)
        part_out[k, chunk:] = split_bias(bias_term)

    def part_copy(i):
        return to_col(part_out.at[col_at(i)], part_in.at[i - 1], part_send.at[i - 1], part_recv.at[i - 1], i)

    for i in range(1, col_count):
        part_copy(i).start()

    self_feat = dot_nt(pre_grad, w_self[...])
    for i in range(1, col_count):
        mean_copy(i).wait_recv()

    def source_part(node):
        total = jnp.zeros((rows, width), f32)
        for k in range(col_count):
            total = total + dot(adj[block(node), k * rows : (k + 1) * rows], mean_all[k])
        return total

    def src_copy(i):
        return to_node(src_out.at[i - 1], src_in.at[i - 1], src_send.at[i - 1], src_recv.at[i - 1], i)

    def send_source(i, _):
        src_out[i - 1] = source_part(node_at(i)).astype(bf16)
        src_copy(i).start()
        return 0

    lax.fori_loop(1, node_count, send_source, 0)

    total = part_out[c, :chunk].astype(f32)
    bias_total = bias_term
    for i in range(1, col_count):
        part_copy(i).wait_recv()
        total = total + part_in[i - 1, :chunk].astype(f32)
        bias_total = bias_total + join_bias(part_in[i - 1, chunk:])
    for k in range(node_count):
        node_out[k, :piece] = total[k * piece : (k + 1) * piece].astype(bf16)
        node_out[k, piece:] = split_bias(bias_total)

    def node_copy(i):
        return to_node(node_out.at[node_at(i)], node_in.at[i - 1], node_send.at[i - 1], node_recv.at[i - 1], i)

    for i in range(1, node_count):
        node_copy(i).start()
    source = source_part(n)
    mine = node_out[n, :piece].astype(f32)
    for i in range(1, node_count):
        node_copy(i).wait_recv()
        mine = mine + node_in[i - 1, :piece].astype(f32)
        bias_total = bias_total + join_bias(node_in[i - 1, piece:])
    bias_grad[...] = bias_total

    own_rows = pl.ds(pl.multiple_of(n * piece, piece), piece)
    full[c, own_rows] = mine.astype(bf16)

    def piece_copy(i):
        return to_node(full.at[c, own_rows], full.at[c, own_rows], piece_send.at[i - 1], piece_recv.at[i - 1], i)

    for i in range(1, node_count):
        piece_copy(i).start()
    for i in range(1, node_count):
        piece_copy(i).wait_recv()

    def full_copy(i):
        return to_col(full.at[c], full.at[c], full_send.at[i - 1], full_recv.at[i - 1], i)

    for i in range(1, col_count):
        full_copy(i).start()

    for i in range(1, node_count):
        src_copy(i).wait_recv()
        source = source + src_in[i - 1].astype(f32)
    to = lax.broadcasted_iota(jnp.int32, (rows, rows), 0)
    frm = lax.broadcasted_iota(jnp.int32, (rows, rows), 1)
    want = (to // 128) * 128 + (to % 8) * 16 + (to % 128) // 8
    order = jnp.where(frm == want, 1.0, 0.0).astype(bf16)
    high = source.astype(bf16)
    low = (source - high.astype(f32)).astype(bf16)
    feat_grad[...] = (self_feat + (dot(order, high) + dot(order, low))).astype(bf16)

    for i in range(1, col_count):
        full_copy(i).wait_recv()
    for k in range(col_count):
        for part in range(chunk // piece):
            row = k * chunk + part * piece
            if row < width:
                self_grad[row : row + piece] = full[k, part * piece : (part + 1) * piece].astype(f32)
            elif row < 2 * width:
                neigh_grad[row - width : row - width + piece] = full[
                    k, part * piece : (part + 1) * piece
                ].astype(f32)
    for i in range(1, col_count):
        sum_copy(i).wait_send()
        mean_copy(i).wait_send()
        part_copy(i).wait_send()
        full_copy(i).wait_send()
    for i in range(1, node_count):
        src_copy(i).wait_send()
        node_copy(i).wait_send()
        piece_copy(i).wait_send()


def layer(sources, adj, deg, feats, w_self, w_neigh, bias, cot, node_count, col_count):
    rows, width = feats.shape
    piece = max(16, 2 * width // (node_count * col_count))
    chunk = node_count * piece
    vmem = pl.BlockSpec(memory_space=pltpu.VMEM)
    bf16, f32 = jnp.bfloat16, jnp.float32
    others, peers = col_count - 1, node_count - 1
    sems = pltpu.SemaphoreType.DMA
    return pl.pallas_call(
        functools.partial(layer_kernel, node_count, col_count, piece),
        out_shape=(
            jax.ShapeDtypeStruct((rows, width), bf16),
            jax.ShapeDtypeStruct((rows, width), bf16),
            jax.ShapeDtypeStruct((width, width), f32),
            jax.ShapeDtypeStruct((width, width), f32),
            jax.ShapeDtypeStruct((1, width), f32),
        ),
        in_specs=[vmem] * (node_count + 7),
        out_specs=(vmem,) * 5,
        scratch_shapes=[
            pltpu.VMEM((others, width + 16, rows), bf16),
            pltpu.VMEM((others, width + 16, rows), bf16),
            pltpu.VMEM((col_count, rows, width), bf16),
            pltpu.VMEM((peers, rows, width), bf16),
            pltpu.VMEM((peers, rows, width), bf16),
            pltpu.VMEM((col_count, chunk + 16, width), bf16),
            pltpu.VMEM((others, chunk + 16, width), bf16),
            pltpu.VMEM((node_count, piece + 16, width), bf16),
            pltpu.VMEM((peers, piece + 16, width), bf16),
            pltpu.VMEM((col_count, chunk, width), bf16),
            sems((others,)), sems((others,)), sems((others,)), sems((others,)),
            sems((peers,)), sems((peers,)), sems((others,)), sems((others,)),
            sems((peers,)), sems((peers,)), sems((peers,)), sems((peers,)),
            sems((others,)), sems((others,)),
        ],
        compiler_params=pltpu.CompilerParams(
            collective_id=0, has_side_effects=True, vmem_limit_bytes=48 * 1024 * 1024
        ),
        cost_estimate=pl.CostEstimate(flops=2_500_000_000, bytes_accessed=9_000_000, transcendentals=70_000),
        name="sage_layer",
    )(*sources, adj, deg, feats, w_self, w_neigh, bias, cot)


def shards(node_feats, tile_row, tile_col, tile_bits, w_self, w_neigh, bias, cotangent):
    rows_dev, width_in = node_feats.shape
    node_count = lax.axis_size("nodes")
    col_count = lax.axis_size("cols")
    per_dev = rows_dev // 128
    ordered = node_feats.reshape(per_dev, 16, 8, width_in).transpose(3, 0, 2, 1).reshape(width_in, rows_dev)
    sources = [ordered]
    for i in range(1, node_count):
        pairs = [(k, (k + i) % node_count) for k in range(node_count)]
        sources.append(lax.ppermute(ordered, "nodes", pairs))
    adj, deg = build(
        tile_row[0], tile_col[0], tile_bits[0], node_count * per_dev, col_count * per_dev
    )
    layer_out, feat_grad, self_grad, neigh_grad, bias_grad = layer(
        sources, adj, deg, node_feats, w_self, w_neigh, bias[None, :], cotangent, node_count, col_count
    )
    return (layer_out, feat_grad, self_grad, neigh_grad, bias_grad[0])


def solution(mesh):
    return jax.shard_map(
        shards,
        mesh=mesh,
        in_specs=(
            P(("nodes", "cols"), None),
            P("nodes", "cols"),
            P("nodes", "cols"),
            P("nodes", "cols", None, None),
            P(),
            P(),
            P(),
            P(("nodes", "cols"), None),
        ),
        out_specs=(P(("nodes", "cols"), None), P(("nodes", "cols"), None), P(), P(), P()),
        check_vma=False,
    )
```

```python
import functools

import jax
import jax.numpy as jnp
from jax import lax
from jax.experimental import pallas as pl
from jax.experimental.pallas import tpu as pltpu
from jax.sharding import PartitionSpec as P


def build_kernel(row_ref, col_ref, bits_hbm, adj_hbm, deg_ref, count_ref, bits_ref, adj_ref, in_sem, out_sem):
    source_count, dest_count = count_ref.shape[:2]
    tile_count = bits_ref.shape[0]
    batch_count = in_sem.shape[0]
    batch = tile_count // batch_count

    def load(k):
        span = pl.ds(k * batch, batch)
        return pltpu.make_async_copy(bits_hbm.at[0, span], bits_ref.at[span], in_sem.at[k])

    for k in range(batch_count):
        load(k).start()
    zero = jnp.zeros((4, 16, 128), jnp.int32)

    def clear(s, _):
        for d in range(dest_count):
            count_ref[s, d] = zero
        return 0

    lax.fori_loop(0, source_count, clear, 0)

    def add_tile(t, _):
        r = row_ref[0, t]
        c = col_ref[0, t]
        word = bits_ref[t]
        spread = word | (word << 12)
        for j in range(4):
            count_ref[c, r, j] += (spread >> j) & 0x10001
        return 0

    for k in range(batch_count):
        load(k).wait()
        lax.fori_loop(k * batch, (k + 1) * batch, add_tile, 0, unroll=4)

    deg_ref[...] = jnp.zeros_like(deg_ref)

    def store(s):
        span = pl.ds(pl.multiple_of(s * 128, 128), 128)
        return pltpu.make_async_copy(adj_ref.at[span], adj_hbm.at[span], out_sem.at[s])

    def expand(s, _):
        for d in range(dest_count):
            lanes = slice(d * 128, (d + 1) * 128)
            total = jnp.zeros((16, 128), jnp.float32)
            for j in range(4):
                pair = count_ref[s, d, j]
                low = (pair & 0xFFFF).astype(jnp.float32)
                high = (pair >> 16).astype(jnp.float32)
                total = total + (low + high)
                adj_ref[pl.ds(s * 128 + j * 16, 16), lanes] = low.astype(jnp.bfloat16)
                adj_ref[pl.ds(s * 128 + (j + 4) * 16, 16), lanes] = high.astype(jnp.bfloat16)
            deg_ref[:, lanes] += total
        store(s).start()
        return 0

    lax.fori_loop(0, source_count, expand, 0)
    for s in range(source_count):
        store(s).wait()


def build(tile_row, tile_col, tile_bits, source_count, dest_count):
    smem = pl.BlockSpec(memory_space=pltpu.SMEM)
    hbm = pl.BlockSpec(memory_space=pltpu.HBM)
    tile_count = tile_row.shape[1]
    batch_count = 4 if tile_count % 16 == 0 else 1
    adj_shape = (source_count * 128, dest_count * 128)
    return pl.pallas_call(
        build_kernel,
        out_shape=(
            jax.ShapeDtypeStruct(adj_shape, jnp.bfloat16),
            jax.ShapeDtypeStruct((16, dest_count * 128), jnp.float32),
        ),
        in_specs=[smem, smem, hbm],
        out_specs=(hbm, pl.BlockSpec(memory_space=pltpu.VMEM)),
        scratch_shapes=[
            pltpu.VMEM((source_count, dest_count, 4, 16, 128), jnp.int32),
            pltpu.VMEM((tile_count, 16, 128), jnp.int32),
            pltpu.VMEM(adj_shape, jnp.bfloat16),
            pltpu.SemaphoreType.DMA((batch_count,)),
            pltpu.SemaphoreType.DMA((source_count,)),
        ],
        compiler_params=pltpu.CompilerParams(vmem_limit_bytes=63 * 1024 * 1024),
        cost_estimate=pl.CostEstimate(flops=20_000_000, bytes_accessed=8_000_000, transcendentals=0),
        name="build_adjacency",
    )(tile_row, tile_col, tile_bits)


def transposed(block):
    return block.astype(jnp.float32).T.astype(block.dtype)


def dot(left, right):
    return jnp.dot(left, right, preferred_element_type=jnp.float32)


def dot_nt(left, right):
    return lax.dot_general(left, right, (((1,), (1,)), ((), ())), preferred_element_type=jnp.float32)


def layer_kernel(node_count, col_count, piece, *refs):
    hbm_in, outs, scratch = refs[:7], refs[7:12], refs[12:]
    (layer_out, feat_grad, self_grad, neigh_grad, bias_grad) = outs
    local, load_sem = scratch[:7], scratch[7]
    (adj, deg, feats, w_self, w_neigh, bias, cot) = local
    (blocks, acc, own_source, sum_out, sum_in, mean_all, src_out, src_in, comb_out, comb_in, part_out, part_in,
     node_out, node_in, full, up_send, down_send, across_send, block_recv, sum_send, sum_recv, mean_send,
     mean_recv, src_send, src_recv, comb_send, comb_recv, part_send, part_recv,
     node_send, node_recv, piece_send, piece_recv, full_send, full_recv) = scratch[8:]
    n = lax.axis_index("nodes")
    c = lax.axis_index("cols")
    rows = feats.shape[0]
    width = feats.shape[1]
    f32, bf16 = jnp.float32, jnp.bfloat16
    length = node_count // 2
    place = lax.div(n, 2)
    side = lax.rem(n, 2)
    partner = place * 2 + 1 - side

    def load(k):
        return pltpu.make_async_copy(hbm_in[k], local[k], load_sem.at[k])

    for k in (2, 0, 1, 3, 4, 5, 6):
        load(k).start()

    def node_at(i):
        return lax.rem(n + i, node_count)

    def col_at(i):
        return lax.rem(c + i, col_count)

    def block(k):
        return pl.ds(pl.multiple_of(k * rows, rows), rows)

    def to_col(src, dst, send, recv, i):
        return pltpu.make_async_remote_copy(
            src_ref=src, dst_ref=dst, send_sem=send, recv_sem=recv,
            device_id=(n, col_at(i)), device_id_type=pl.DeviceIdType.MESH)

    def to_node(src, dst, send, recv, i):
        return pltpu.make_async_remote_copy(
            src_ref=src, dst_ref=dst, send_sem=send, recv_sem=recv,
            device_id=(node_at(i), c), device_id_type=pl.DeviceIdType.MESH)

    def to_device(src, dst, send, recv, node):
        return pltpu.make_async_remote_copy(
            src_ref=src, dst_ref=dst, send_sem=send, recv_sem=recv,
            device_id=(node, c), device_id_type=pl.DeviceIdType.MESH)

    barrier = pltpu.get_barrier_semaphore()
    for i in range(1, col_count):
        pl.semaphore_signal(barrier, inc=1, device_id=(n, col_at(i)), device_id_type=pl.DeviceIdType.MESH)
    for i in range(1, node_count):
        pl.semaphore_signal(barrier, inc=1, device_id=(node_at(i), c), device_id_type=pl.DeviceIdType.MESH)
    pl.semaphore_wait(barrier, col_count + node_count - 2)

    to = lax.broadcasted_iota(jnp.int32, (rows, rows), 0)
    frm = lax.broadcasted_iota(jnp.int32, (rows, rows), 1)
    want = (to // 128) * 128 + (to % 8) * 16 + (to % 128) // 8
    order = jnp.where(frm == want, 1.0, 0.0).astype(bf16)

    def up(b):
        return to_device(blocks.at[b], blocks.at[b], up_send.at[b], block_recv.at[b], n + 2)

    def down(b):
        return to_device(blocks.at[b], blocks.at[b], down_send.at[b], block_recv.at[b], n - 2)

    def across(b):
        return to_device(blocks.at[b], blocks.at[b], across_send.at[b], block_recv.at[b], partner)

    def accumulate(b):
        acc[...] += dot(blocks[b], adj[block(b), :])

    load(2).wait()
    feats_t = transposed(feats[...])
    blocks[n] = dot(feats_t, order).astype(bf16)

    @pl.when(place + 1 < length)
    def _():
        up(n).start()

    @pl.when(place > 0)
    def _():
        down(n).start()

    across(n).start()
    load(0).wait()
    acc[...] = dot(blocks[n], adj[block(n), :])

    def along(d, _):
        @pl.when(place - d >= 0)
        def _():
            b = n - 2 * d
            across(b).wait_recv()

            @pl.when(place + 1 < length)
            def _():
                up(b).start()

            across(b).start()

        @pl.when(place + d < length)
        def _():
            b = n + 2 * d
            across(b).wait_recv()

            @pl.when(place > 0)
            def _():
                down(b).start()

            across(b).start()

        @pl.when(place - d >= 0)
        def _():
            accumulate(n - 2 * d)

        @pl.when(place + d < length)
        def _():
            accumulate(n + 2 * d)

        return 0

    lax.fori_loop(1, length, along, 0)
    for k in (1, 3, 4, 5, 6):
        load(k).wait()
    self_act = dot(feats[...], w_self[...]) + bias[...]

    def opposite(d, _):
        @pl.when(place - d >= 0)
        def _():
            across(partner - 2 * d).wait_recv()
            accumulate(partner - 2 * d)

        @pl.when((place + d < length) & (d > 0))
        def _():
            across(partner + 2 * d).wait_recv()
            accumulate(partner + 2 * d)

        return 0

    lax.fori_loop(0, length, opposite, 0)

    def part_sum(col):
        return acc[:, block(col)]

    def part_degree(col):
        return jnp.sum(deg[:, block(col)], axis=0, keepdims=True)

    def sum_copy(i):
        return to_col(sum_out.at[i - 1], sum_in.at[i - 1], sum_send.at[i - 1], sum_recv.at[i - 1], i)

    first = lax.broadcasted_iota(jnp.int32, (16, rows), 0) == 0

    def send_sum(i, _):
        col = col_at(i)
        sum_out[i - 1, :width] = part_sum(col).astype(bf16)
        degree = part_degree(col)
        high = jnp.floor(degree * (1.0 / 256.0))
        low = degree - high * 256.0
        sum_out[i - 1, width:] = jnp.where(first, high, low).astype(bf16)
        sum_copy(i).start()
        return 0

    lax.fori_loop(1, col_count, send_sum, 0)
    summed = part_sum(c)
    degree = part_degree(c)
    for i in range(1, col_count):
        sum_copy(i).wait_recv()
        summed = summed + sum_in[i - 1, :width].astype(f32)
        tail = sum_in[i - 1, width:].astype(f32)
        degree = degree + tail[0:1] * 256.0 + tail[1:2]
    degree = jnp.maximum(degree, 1.0)

    mean_t = summed / degree
    mean = mean_t.T.astype(bf16)
    mean_t = mean_t.astype(bf16)
    preact = self_act + dot(mean, w_neigh[...])
    gate = jax.nn.sigmoid(preact)
    layer_out[...] = (preact * gate).astype(bf16)
    pre_grad = (cot[...].astype(f32) * gate * (1.0 + preact * (1.0 - gate))).astype(bf16)
    mean_grad = dot_nt(w_neigh[...], pre_grad) / degree
    mean_all[c] = mean_grad.T.astype(bf16)

    def mean_copy(i):
        return to_col(mean_all.at[c], mean_all.at[c], mean_send.at[i - 1], mean_recv.at[i - 1], i)

    for i in range(1, col_count):
        mean_copy(i).start()

    self_term = dot(feats_t, pre_grad)
    neigh_term = dot(mean_t, pre_grad)
    bias_term = jnp.sum(pre_grad.astype(f32), axis=0, keepdims=True)
    chunk = node_count * piece
    top = lax.broadcasted_iota(jnp.int32, (16, width), 0) == 0

    def split_bias(value):
        high = value.astype(bf16).astype(f32)
        return jnp.where(top, high, value - high).astype(bf16)

    def join_bias(value):
        pair = value.astype(f32)
        return pair[0:1] + pair[1:2]

    terms = jnp.concatenate([self_term, neigh_term], axis=0)
    spare = col_count * chunk - 2 * width
    if spare:
        terms = jnp.concatenate([terms, jnp.zeros((spare, width), f32)], axis=0)
    for k in range(col_count):
        part_out[k, :chunk] = terms[k * chunk : (k + 1) * chunk].astype(bf16)
        part_out[k, chunk:] = split_bias(bias_term)

    def part_copy(i):
        return to_col(part_out.at[col_at(i)], part_in.at[i - 1], part_send.at[i - 1], part_recv.at[i - 1], i)

    for i in range(1, col_count):
        part_copy(i).start()

    self_feat = dot_nt(pre_grad, w_self[...])
    for i in range(1, col_count):
        mean_copy(i).wait_recv()

    def source_part(node):
        total = jnp.zeros((rows, width), f32)
        for k in range(col_count):
            total = total + dot(adj[block(node), k * rows : (k + 1) * rows], mean_all[k])
        return total

    def goal(i):
        return jnp.where(place * 2 < length, length - 1 - i, i)

    def src_copy(i):
        return to_device(src_out.at[i], src_in.at[i], src_send.at[i], src_recv.at[i], partner)

    def comb_copy(i, sender):
        return to_device(comb_out.at[i], comb_in.at[sender], comb_send.at[i], comb_recv.at[sender], goal(i) * 2 + side)

    def send_source(i, _):
        src_out[i] = source_part(goal(i) * 2 + 1 - side).astype(bf16)
        src_copy(i).start()
        return 0

    lax.fori_loop(0, length, send_source, 0)

    total = part_out[c, :chunk].astype(f32)
    bias_total = bias_term
    for i in range(1, col_count):
        part_copy(i).wait_recv()
        total = total + part_in[i - 1, :chunk].astype(f32)
        bias_total = bias_total + join_bias(part_in[i - 1, chunk:])
    for k in range(node_count):
        node_out[k, :piece] = total[k * piece : (k + 1) * piece].astype(bf16)
        node_out[k, piece:] = split_bias(bias_total)

    def node_copy(i):
        return to_node(node_out.at[node_at(i)], node_in.at[i - 1], node_send.at[i - 1], node_recv.at[i - 1], i)

    for i in range(1, node_count):
        node_copy(i).start()

    def combine(i, _):
        part = source_part(goal(i) * 2 + side)
        src_copy(i).wait_recv()
        part = part + src_in[i].astype(f32)

        @pl.when(goal(i) != place)
        def _():
            comb_out[i] = part.astype(bf16)
            comb_copy(i, place).start()

        @pl.when(goal(i) == place)
        def _():
            own_source[...] = part

        return 0

    lax.fori_loop(0, length, combine, 0)
    mine = node_out[n, :piece].astype(f32)
    for i in range(1, node_count):
        node_copy(i).wait_recv()
        mine = mine + node_in[i - 1, :piece].astype(f32)
        bias_total = bias_total + join_bias(node_in[i - 1, piece:])
    bias_grad[...] = bias_total

    own_rows = pl.ds(pl.multiple_of(n * piece, piece), piece)
    full[c, own_rows] = mine.astype(bf16)

    def piece_copy(i):
        return to_node(full.at[c, own_rows], full.at[c, own_rows], piece_send.at[i - 1], piece_recv.at[i - 1], i)

    for i in range(1, node_count):
        piece_copy(i).start()
    for i in range(1, node_count):
        piece_copy(i).wait_recv()

    def full_copy(i):
        return to_col(full.at[c], full.at[c], full_send.at[i - 1], full_recv.at[i - 1], i)

    for i in range(1, col_count):
        full_copy(i).start()

    def collect(j, _):
        @pl.when(j != place)
        def _():
            comb_copy(0, j).wait_recv()
            own_source[...] += comb_in[j].astype(f32)

        return 0

    lax.fori_loop(0, length, collect, 0)
    source = own_source[...]
    high = source.astype(bf16)
    low = (source - high.astype(f32)).astype(bf16)
    feat_grad[...] = (self_feat + (dot(order, high) + dot(order, low))).astype(bf16)

    for i in range(1, col_count):
        full_copy(i).wait_recv()
    for k in range(col_count):
        for part in range(chunk // piece):
            row = k * chunk + part * piece
            if row < width:
                self_grad[row : row + piece] = full[k, part * piece : (part + 1) * piece].astype(f32)
            elif row < 2 * width:
                neigh_grad[row - width : row - width + piece] = full[
                    k, part * piece : (part + 1) * piece
                ].astype(f32)
    for i in range(1, col_count):
        sum_copy(i).wait_send()
        mean_copy(i).wait_send()
        part_copy(i).wait_send()
        full_copy(i).wait_send()

    def drain(i, _):
        src_copy(i).wait_send()
        across(i * 2 + side).wait_send()

        @pl.when(goal(i) != place)
        def _():
            comb_copy(i, place).wait_send()

        @pl.when((i <= place) & (place + 1 < length))
        def _():
            up(i * 2 + side).wait_send()

        @pl.when((i >= place) & (place > 0))
        def _():
            down(i * 2 + side).wait_send()

        return 0

    lax.fori_loop(0, length, drain, 0)
    for i in range(1, node_count):
        node_copy(i).wait_send()
        piece_copy(i).wait_send()


def layer(adj, deg, feats, w_self, w_neigh, bias, cot, node_count, col_count):
    rows, width = feats.shape
    piece = max(16, 2 * width // (node_count * col_count))
    chunk = node_count * piece
    vmem = pl.BlockSpec(memory_space=pltpu.VMEM)
    hbm = pl.BlockSpec(memory_space=pltpu.HBM)
    inputs = (adj, deg, feats, w_self, w_neigh, bias, cot)
    length = node_count // 2
    bf16, f32 = jnp.bfloat16, jnp.float32
    others, peers = col_count - 1, node_count - 1
    sems = pltpu.SemaphoreType.DMA
    return pl.pallas_call(
        functools.partial(layer_kernel, node_count, col_count, piece),
        out_shape=(
            jax.ShapeDtypeStruct((rows, width), bf16),
            jax.ShapeDtypeStruct((rows, width), bf16),
            jax.ShapeDtypeStruct((width, width), f32),
            jax.ShapeDtypeStruct((width, width), f32),
            jax.ShapeDtypeStruct((1, width), f32),
        ),
        in_specs=[hbm] * 7,
        out_specs=(vmem,) * 5,
        scratch_shapes=[
            *[pltpu.VMEM(x.shape, x.dtype) for x in inputs],
            sems((7,)),
            pltpu.VMEM((node_count, width, rows), bf16),
            pltpu.VMEM((width, col_count * rows), f32),
            pltpu.VMEM((rows, width), f32),
            pltpu.VMEM((others, width + 16, rows), bf16),
            pltpu.VMEM((others, width + 16, rows), bf16),
            pltpu.VMEM((col_count, rows, width), bf16),
            pltpu.VMEM((length, rows, width), bf16),
            pltpu.VMEM((length, rows, width), bf16),
            pltpu.VMEM((length, rows, width), bf16),
            pltpu.VMEM((length, rows, width), bf16),
            pltpu.VMEM((col_count, chunk + 16, width), bf16),
            pltpu.VMEM((others, chunk + 16, width), bf16),
            pltpu.VMEM((node_count, piece + 16, width), bf16),
            pltpu.VMEM((peers, piece + 16, width), bf16),
            pltpu.VMEM((col_count, chunk, width), bf16),
            sems((node_count,)), sems((node_count,)), sems((node_count,)), sems((node_count,)),
            sems((others,)), sems((others,)), sems((others,)), sems((others,)),
            sems((length,)), sems((length,)), sems((length,)), sems((length,)),
            sems((others,)), sems((others,)),
            sems((peers,)), sems((peers,)), sems((peers,)), sems((peers,)),
            sems((others,)), sems((others,)),
        ],
        compiler_params=pltpu.CompilerParams(
            collective_id=0, has_side_effects=True, vmem_limit_bytes=63 * 1024 * 1024
        ),
        cost_estimate=pl.CostEstimate(flops=2_500_000_000, bytes_accessed=9_000_000, transcendentals=70_000),
        name="sage_layer",
    )(*inputs)


def finish_kernel(*refs):
    copies = [pltpu.make_async_copy(refs[k], refs[5 + k], refs[10].at[k]) for k in range(5)]
    for copy in copies:
        copy.start()
    for copy in copies:
        copy.wait()


def finish(results):
    hbm = pl.BlockSpec(memory_space=pltpu.HBM)
    return pl.pallas_call(
        finish_kernel,
        out_shape=tuple(jax.ShapeDtypeStruct(x.shape, x.dtype) for x in results),
        in_specs=[hbm] * 5,
        out_specs=(hbm,) * 5,
        scratch_shapes=[pltpu.SemaphoreType.DMA((5,))],
        compiler_params=pltpu.CompilerParams(vmem_limit_bytes=63 * 1024 * 1024),
        name="write_results",
    )(*results)


def shards(node_feats, tile_row, tile_col, tile_bits, w_self, w_neigh, bias, cotangent):
    rows_dev, width_in = node_feats.shape
    node_count = lax.axis_size("nodes")
    col_count = lax.axis_size("cols")
    per_dev = rows_dev // 128
    adj, deg = build(tile_row, tile_col, tile_bits, node_count * per_dev, col_count * per_dev)
    layer_out, feat_grad, self_grad, neigh_grad, bias_grad = finish(
        layer(adj, deg, node_feats, w_self, w_neigh, bias[None, :], cotangent, node_count, col_count)
    )
    return (layer_out, feat_grad, self_grad, neigh_grad, bias_grad[0])


def solution(mesh):
    return jax.shard_map(
        shards,
        mesh=mesh,
        in_specs=(
            P(("nodes", "cols"), None),
            P("nodes", "cols"),
            P("nodes", "cols"),
            P("nodes", "cols", None, None),
            P(),
            P(),
            P(),
            P(("nodes", "cols"), None),
        ),
        out_specs=(P(("nodes", "cols"), None), P(("nodes", "cols"), None), P(), P(), P()),
        check_vma=False,
    )
```

```python
import functools

import jax
import jax.numpy as jnp
from jax import lax
from jax.experimental import pallas as pl
from jax.experimental.pallas import tpu as pltpu
from jax.sharding import PartitionSpec as P


def build_kernel(row_ref, col_ref, bits_hbm, adj_hbm, deg_ref, count_ref, bits_ref, adj_ref, in_sem, out_sem):
    source_count, dest_count = count_ref.shape[:2]
    tile_count = bits_ref.shape[0]
    batch_count = in_sem.shape[0]
    batch = tile_count // batch_count

    def load(k):
        span = pl.ds(k * batch, batch)
        return pltpu.make_async_copy(bits_hbm.at[0, span], bits_ref.at[span], in_sem.at[k])

    for k in range(batch_count):
        load(k).start()
    zero = jnp.zeros((4, 16, 128), jnp.int32)

    def clear(s, _):
        for d in range(dest_count):
            count_ref[s, d] = zero
        return 0

    lax.fori_loop(0, source_count, clear, 0)

    def add_tile(t, _):
        r = row_ref[0, t]
        c = col_ref[0, t]
        word = bits_ref[t]
        spread = word | (word << 12)
        for j in range(4):
            count_ref[c, r, j] += (spread >> j) & 0x10001
        return 0

    for k in range(batch_count):
        load(k).wait()
        lax.fori_loop(k * batch, (k + 1) * batch, add_tile, 0, unroll=4)

    deg_ref[...] = jnp.zeros_like(deg_ref)

    def store(s):
        span = pl.ds(pl.multiple_of(s * 128, 128), 128)
        return pltpu.make_async_copy(adj_ref.at[span], adj_hbm.at[span], out_sem.at[s])

    def expand(s, _):
        for d in range(dest_count):
            lanes = slice(d * 128, (d + 1) * 128)
            total = jnp.zeros((16, 128), jnp.float32)
            for j in range(4):
                pair = count_ref[s, d, j]
                low = (pair & 0xFFFF).astype(jnp.float32)
                high = (pair >> 16).astype(jnp.float32)
                total = total + (low + high)
                adj_ref[pl.ds(s * 128 + j * 16, 16), lanes] = low.astype(jnp.bfloat16)
                adj_ref[pl.ds(s * 128 + (j + 4) * 16, 16), lanes] = high.astype(jnp.bfloat16)
            deg_ref[:, lanes] += total
        store(s).start()
        return 0

    lax.fori_loop(0, source_count, expand, 0)
    for s in range(source_count):
        store(s).wait()


def build(tile_row, tile_col, tile_bits, source_count, dest_count):
    smem = pl.BlockSpec(memory_space=pltpu.SMEM)
    hbm = pl.BlockSpec(memory_space=pltpu.HBM)
    tile_count = tile_row.shape[1]
    batch_count = 4 if tile_count % 16 == 0 else 1
    adj_shape = (source_count * 128, dest_count * 128)
    return pl.pallas_call(
        build_kernel,
        out_shape=(
            jax.ShapeDtypeStruct(adj_shape, jnp.bfloat16),
            jax.ShapeDtypeStruct((16, dest_count * 128), jnp.float32),
        ),
        in_specs=[smem, smem, hbm],
        out_specs=(hbm, pl.BlockSpec(memory_space=pltpu.VMEM)),
        scratch_shapes=[
            pltpu.VMEM((source_count, dest_count, 4, 16, 128), jnp.int32),
            pltpu.VMEM((tile_count, 16, 128), jnp.int32),
            pltpu.VMEM(adj_shape, jnp.bfloat16),
            pltpu.SemaphoreType.DMA((batch_count,)),
            pltpu.SemaphoreType.DMA((source_count,)),
        ],
        compiler_params=pltpu.CompilerParams(vmem_limit_bytes=63 * 1024 * 1024),
        cost_estimate=pl.CostEstimate(flops=20_000_000, bytes_accessed=8_000_000, transcendentals=0),
        name="build_adjacency",
    )(tile_row, tile_col, tile_bits)


def transposed(block):
    return block.astype(jnp.float32).T.astype(block.dtype)


def dot(left, right):
    return jnp.dot(left, right, preferred_element_type=jnp.float32)


def dot_nt(left, right):
    return lax.dot_general(left, right, (((1,), (1,)), ((), ())), preferred_element_type=jnp.float32)


def layer_kernel(node_count, col_count, piece, *refs):
    hbm_in, outs, scratch = refs[:7], refs[7:12], refs[12:]
    (layer_out, feat_grad, self_grad, neigh_grad, bias_grad) = outs
    local, load_sem = scratch[:7], scratch[7]
    (adj, deg, feats, w_self, w_neigh, bias, cot) = local
    (blocks, acc, own_source, sib_out, sib_in, sum_out, sum_in, mean_all, src_out, src_in, comb_out, comb_in, part_out, part_in,
     node_out, node_in, full, up_send, down_send, across_send, block_recv, sib_send, sib_recv, sum_send, sum_recv,
     mean_send, mean_recv, pass_send, src_send, src_recv, comb_send, comb_recv, part_send, part_recv,
     node_send, node_recv, piece_send, piece_recv, full_send, full_recv) = scratch[8:]
    n = lax.axis_index("nodes")
    c = lax.axis_index("cols")
    rows = feats.shape[0]
    width = feats.shape[1]
    f32, bf16 = jnp.float32, jnp.bfloat16
    length = node_count // 2
    place = lax.div(n, 2)
    side = lax.rem(n, 2)
    partner = place * 2 + 1 - side

    def load(k):
        return pltpu.make_async_copy(hbm_in[k], local[k], load_sem.at[k])

    for k in (2, 0, 1, 3, 4, 5, 6):
        load(k).start()

    def node_at(i):
        return lax.rem(n + i, node_count)

    def col_at(i):
        return lax.rem(c + i, col_count)

    def block(k):
        return pl.ds(pl.multiple_of(k * rows, rows), rows)

    def to_col(src, dst, send, recv, i):
        return pltpu.make_async_remote_copy(
            src_ref=src, dst_ref=dst, send_sem=send, recv_sem=recv,
            device_id=(n, col_at(i)), device_id_type=pl.DeviceIdType.MESH)

    def to_node(src, dst, send, recv, i):
        return pltpu.make_async_remote_copy(
            src_ref=src, dst_ref=dst, send_sem=send, recv_sem=recv,
            device_id=(node_at(i), c), device_id_type=pl.DeviceIdType.MESH)

    pairs = col_count // 2
    core = lax.rem(c, 2)
    line = lax.div(c, 2)

    def col_of(i, k):
        return lax.rem(line + i, pairs) * 2 + k

    def to_sibling(src, dst, send, recv):
        return pltpu.make_async_remote_copy(
            src_ref=src, dst_ref=dst, send_sem=send, recv_sem=recv,
            device_id=(n, line * 2 + 1 - core), device_id_type=pl.DeviceIdType.MESH)

    def to_peer(src, dst, send, recv, i):
        return pltpu.make_async_remote_copy(
            src_ref=src, dst_ref=dst, send_sem=send, recv_sem=recv,
            device_id=(n, col_of(i, core)), device_id_type=pl.DeviceIdType.MESH)

    def to_device(src, dst, send, recv, node):
        return pltpu.make_async_remote_copy(
            src_ref=src, dst_ref=dst, send_sem=send, recv_sem=recv,
            device_id=(node, c), device_id_type=pl.DeviceIdType.MESH)

    barrier = pltpu.get_barrier_semaphore()
    for i in range(1, col_count):
        pl.semaphore_signal(barrier, inc=1, device_id=(n, col_at(i)), device_id_type=pl.DeviceIdType.MESH)
    for i in range(1, node_count):
        pl.semaphore_signal(barrier, inc=1, device_id=(node_at(i), c), device_id_type=pl.DeviceIdType.MESH)
    pl.semaphore_wait(barrier, col_count + node_count - 2)

    to = lax.broadcasted_iota(jnp.int32, (rows, rows), 0)
    frm = lax.broadcasted_iota(jnp.int32, (rows, rows), 1)
    want = (to // 128) * 128 + (to % 8) * 16 + (to % 128) // 8
    order = jnp.where(frm == want, 1.0, 0.0).astype(bf16)

    def up(b):
        return to_device(blocks.at[b], blocks.at[b], up_send.at[b], block_recv.at[b], n + 2)

    def down(b):
        return to_device(blocks.at[b], blocks.at[b], down_send.at[b], block_recv.at[b], n - 2)

    def across(b):
        return to_device(blocks.at[b], blocks.at[b], across_send.at[b], block_recv.at[b], partner)

    def accumulate(b):
        acc[...] += dot(blocks[b], adj[block(b), :])

    load(2).wait()
    feats_t = transposed(feats[...])
    blocks[n] = dot(feats_t, order).astype(bf16)

    @pl.when(place + 1 < length)
    def _():
        up(n).start()

    @pl.when(place > 0)
    def _():
        down(n).start()

    across(n).start()
    load(0).wait()
    acc[...] = dot(blocks[n], adj[block(n), :])

    def along(d, _):
        @pl.when(place - d >= 0)
        def _():
            b = n - 2 * d
            across(b).wait_recv()

            @pl.when(place + 1 < length)
            def _():
                up(b).start()

            across(b).start()

        @pl.when(place + d < length)
        def _():
            b = n + 2 * d
            across(b).wait_recv()

            @pl.when(place > 0)
            def _():
                down(b).start()

            across(b).start()

        @pl.when(place - d >= 0)
        def _():
            accumulate(n - 2 * d)

        @pl.when(place + d < length)
        def _():
            accumulate(n + 2 * d)

        return 0

    lax.fori_loop(1, length, along, 0)
    for k in (1, 3, 4, 5, 6):
        load(k).wait()
    self_act = dot(feats[...], w_self[...]) + bias[...]

    def opposite(d, _):
        @pl.when(place - d >= 0)
        def _():
            across(partner - 2 * d).wait_recv()
            accumulate(partner - 2 * d)

        @pl.when((place + d < length) & (d > 0))
        def _():
            across(partner + 2 * d).wait_recv()
            accumulate(partner + 2 * d)

        return 0

    lax.fori_loop(0, length, opposite, 0)

    def part_sum(col):
        return acc[:, block(col)]

    def part_degree(col):
        return jnp.sum(deg[:, block(col)], axis=0, keepdims=True)

    def sib_copy(i):
        return to_sibling(sib_out.at[i], sib_in.at[i], sib_send.at[i], sib_recv.at[i])

    def sum_copy(i):
        return to_peer(sum_out.at[i - 1], sum_in.at[i - 1], sum_send.at[i - 1], sum_recv.at[i - 1], i)

    digit = lax.broadcasted_iota(jnp.int32, (16, rows), 0)

    def pack(ref, slot, part, degree):
        high = jnp.floor(degree * (1.0 / 65536.0))
        rest = degree - high * 65536.0
        middle = jnp.floor(rest * (1.0 / 256.0))
        low = rest - middle * 256.0
        ref[slot, :width] = part.astype(bf16)
        ref[slot, width:] = jnp.where(digit == 0, high, jnp.where(digit == 1, middle, low)).astype(bf16)

    def unpack(ref, slot):
        tail = ref[slot, width:].astype(f32)
        return ref[slot, :width].astype(f32), tail[0:1] * 65536.0 + tail[1:2] * 256.0 + tail[2:3]

    for i in (*range(1, pairs), 0):
        col = col_of(i, 1 - core)
        pack(sib_out, i, part_sum(col), part_degree(col))
        sib_copy(i).start()
    for i in range(1, pairs):
        col = col_of(i, core)
        sib_copy(i).wait_recv()
        part, part_deg = unpack(sib_in, i)
        pack(sum_out, i - 1, part + part_sum(col), part_deg + part_degree(col))
        sum_copy(i).start()
    sib_copy(0).wait_recv()
    part, part_deg = unpack(sib_in, 0)
    summed = part + part_sum(c)
    degree = part_deg + part_degree(c)
    for i in range(1, pairs):
        sum_copy(i).wait_recv()
        part, part_deg = unpack(sum_in, i - 1)
        summed = summed + part
        degree = degree + part_deg
    degree = jnp.maximum(degree, 1.0)

    mean_t = summed / degree
    mean = mean_t.T.astype(bf16)
    mean_t = mean_t.astype(bf16)
    preact = self_act + dot(mean, w_neigh[...])
    gate = jax.nn.sigmoid(preact)
    layer_out[...] = (preact * gate).astype(bf16)
    pre_grad = (cot[...].astype(f32) * gate * (1.0 + preact * (1.0 - gate))).astype(bf16)
    mean_grad = dot_nt(w_neigh[...], pre_grad) / degree
    mean_all[block(c)] = mean_grad.T.astype(bf16)

    def mean_peer(i):
        held = mean_all.at[block(c)]
        return to_peer(held, held, mean_send.at[i - 1], mean_recv.at[c], i)

    def mean_sibling(i, k):
        held = mean_all.at[block(col_of(i, k))]
        return to_sibling(held, held, pass_send.at[i], mean_recv.at[col_of(i, k)])

    for i in range(1, pairs):
        mean_peer(i).start()
    mean_sibling(0, core).start()

    self_term = dot(feats_t, pre_grad)
    neigh_term = dot(mean_t, pre_grad)
    bias_term = jnp.sum(pre_grad.astype(f32), axis=0, keepdims=True)
    chunk = node_count * piece
    top = lax.broadcasted_iota(jnp.int32, (16, width), 0) == 0

    def split_bias(value):
        high = value.astype(bf16).astype(f32)
        return jnp.where(top, high, value - high).astype(bf16)

    def join_bias(value):
        pair = value.astype(f32)
        return pair[0:1] + pair[1:2]

    terms = jnp.concatenate([self_term, neigh_term], axis=0)
    spare = col_count * chunk - 2 * width
    if spare:
        terms = jnp.concatenate([terms, jnp.zeros((spare, width), f32)], axis=0)
    for k in range(col_count):
        part_out[k, :chunk] = terms[k * chunk : (k + 1) * chunk].astype(bf16)
        part_out[k, chunk:] = split_bias(bias_term)

    def part_copy(i):
        return to_col(part_out.at[col_at(i)], part_in.at[i - 1], part_send.at[i - 1], part_recv.at[i - 1], i)

    for i in range(1, col_count):
        part_copy(i).start()

    self_feat = dot_nt(pre_grad, w_self[...])
    for i in range(1, pairs):
        mean_sibling(i, core).wait_recv()
        mean_sibling(i, core).start()
    for i in range(pairs):
        mean_sibling(i, 1 - core).wait_recv()

    def source_part(node):
        return dot(adj[block(node), :], mean_all[...])

    def goal(i):
        return jnp.where(place * 2 < length, length - 1 - i, i)

    def src_copy(i):
        return to_device(src_out.at[i], src_in.at[i], src_send.at[i], src_recv.at[i], partner)

    def comb_copy(i, sender):
        return to_device(comb_out.at[i], comb_in.at[sender], comb_send.at[i], comb_recv.at[sender], goal(i) * 2 + side)

    def send_source(i, _):
        src_out[i] = source_part(goal(i) * 2 + 1 - side).astype(bf16)
        src_copy(i).start()
        return 0

    lax.fori_loop(0, length, send_source, 0)

    total = part_out[c, :chunk].astype(f32)
    bias_total = bias_term
    for i in range(1, col_count):
        part_copy(i).wait_recv()
        total = total + part_in[i - 1, :chunk].astype(f32)
        bias_total = bias_total + join_bias(part_in[i - 1, chunk:])
    for k in range(node_count):
        node_out[k, :piece] = total[k * piece : (k + 1) * piece].astype(bf16)
        node_out[k, piece:] = split_bias(bias_total)

    def node_copy(i):
        return to_node(node_out.at[node_at(i)], node_in.at[i - 1], node_send.at[i - 1], node_recv.at[i - 1], i)

    for i in range(1, node_count):
        node_copy(i).start()

    def combine(i, _):
        part = source_part(goal(i) * 2 + side)
        src_copy(i).wait_recv()
        part = part + src_in[i].astype(f32)

        @pl.when(goal(i) != place)
        def _():
            comb_out[i] = part.astype(bf16)
            comb_copy(i, place).start()

        @pl.when(goal(i) == place)
        def _():
            own_source[...] = part

        return 0

    lax.fori_loop(0, length, combine, 0)
    mine = node_out[n, :piece].astype(f32)
    for i in range(1, node_count):
        node_copy(i).wait_recv()
        mine = mine + node_in[i - 1, :piece].astype(f32)
        bias_total = bias_total + join_bias(node_in[i - 1, piece:])
    bias_grad[...] = bias_total

    own_rows = pl.ds(pl.multiple_of(n * piece, piece), piece)
    full[c, own_rows] = mine.astype(bf16)

    def piece_copy(i):
        return to_node(full.at[c, own_rows], full.at[c, own_rows], piece_send.at[i - 1], piece_recv.at[i - 1], i)

    for i in range(1, node_count):
        piece_copy(i).start()
    for i in range(1, node_count):
        piece_copy(i).wait_recv()

    def full_copy(i):
        return to_col(full.at[c], full.at[c], full_send.at[i - 1], full_recv.at[i - 1], i)

    for i in range(1, col_count):
        full_copy(i).start()

    def collect(j, _):
        @pl.when(j != place)
        def _():
            comb_copy(0, j).wait_recv()
            own_source[...] += comb_in[j].astype(f32)

        return 0

    lax.fori_loop(0, length, collect, 0)
    source = own_source[...]
    high = source.astype(bf16)
    low = (source - high.astype(f32)).astype(bf16)
    feat_grad[...] = (self_feat + (dot(order, high) + dot(order, low))).astype(bf16)

    for i in range(1, col_count):
        full_copy(i).wait_recv()
    for k in range(col_count):
        for part in range(chunk // piece):
            row = k * chunk + part * piece
            if row < width:
                self_grad[row : row + piece] = full[k, part * piece : (part + 1) * piece].astype(f32)
            elif row < 2 * width:
                neigh_grad[row - width : row - width + piece] = full[
                    k, part * piece : (part + 1) * piece
                ].astype(f32)
    for i in range(1, col_count):
        part_copy(i).wait_send()
        full_copy(i).wait_send()

    for i in range(1, pairs):
        sum_copy(i).wait_send()
        mean_peer(i).wait_send()
    for i in range(pairs):
        sib_copy(i).wait_send()
        mean_sibling(i, core).wait_send()

    def drain(i, _):
        src_copy(i).wait_send()
        across(i * 2 + side).wait_send()

        @pl.when(goal(i) != place)
        def _():
            comb_copy(i, place).wait_send()

        @pl.when((i <= place) & (place + 1 < length))
        def _():
            up(i * 2 + side).wait_send()

        @pl.when((i >= place) & (place > 0))
        def _():
            down(i * 2 + side).wait_send()

        return 0

    lax.fori_loop(0, length, drain, 0)
    for i in range(1, node_count):
        node_copy(i).wait_send()
        piece_copy(i).wait_send()


def layer(adj, deg, feats, w_self, w_neigh, bias, cot, node_count, col_count):
    rows, width = feats.shape
    piece = max(16, 2 * width // (node_count * col_count))
    chunk = node_count * piece
    vmem = pl.BlockSpec(memory_space=pltpu.VMEM)
    hbm = pl.BlockSpec(memory_space=pltpu.HBM)
    inputs = (adj, deg, feats, w_self, w_neigh, bias, cot)
    length = node_count // 2
    pairs = col_count // 2
    bf16, f32 = jnp.bfloat16, jnp.float32
    others, peers = col_count - 1, node_count - 1
    sems = pltpu.SemaphoreType.DMA
    return pl.pallas_call(
        functools.partial(layer_kernel, node_count, col_count, piece),
        out_shape=(
            jax.ShapeDtypeStruct((rows, width), bf16),
            jax.ShapeDtypeStruct((rows, width), bf16),
            jax.ShapeDtypeStruct((width, width), f32),
            jax.ShapeDtypeStruct((width, width), f32),
            jax.ShapeDtypeStruct((1, width), f32),
        ),
        in_specs=[hbm] * 7,
        out_specs=(vmem,) * 5,
        scratch_shapes=[
            *[pltpu.VMEM(x.shape, x.dtype) for x in inputs],
            sems((7,)),
            pltpu.VMEM((node_count, width, rows), bf16),
            pltpu.VMEM((width, col_count * rows), f32),
            pltpu.VMEM((rows, width), f32),
            pltpu.VMEM((pairs, width + 16, rows), bf16),
            pltpu.VMEM((pairs, width + 16, rows), bf16),
            pltpu.VMEM((pairs - 1, width + 16, rows), bf16),
            pltpu.VMEM((pairs - 1, width + 16, rows), bf16),
            pltpu.VMEM((col_count * rows, width), bf16),
            pltpu.VMEM((length, rows, width), bf16),
            pltpu.VMEM((length, rows, width), bf16),
            pltpu.VMEM((length, rows, width), bf16),
            pltpu.VMEM((length, rows, width), bf16),
            pltpu.VMEM((col_count, chunk + 16, width), bf16),
            pltpu.VMEM((others, chunk + 16, width), bf16),
            pltpu.VMEM((node_count, piece + 16, width), bf16),
            pltpu.VMEM((peers, piece + 16, width), bf16),
            pltpu.VMEM((col_count, chunk, width), bf16),
            sems((node_count,)), sems((node_count,)), sems((node_count,)), sems((node_count,)),
            sems((pairs,)), sems((pairs,)), sems((pairs - 1,)), sems((pairs - 1,)),
            sems((pairs - 1,)), sems((col_count,)), sems((pairs,)),
            sems((length,)), sems((length,)), sems((length,)), sems((length,)),
            sems((others,)), sems((others,)),
            sems((peers,)), sems((peers,)), sems((peers,)), sems((peers,)),
            sems((others,)), sems((others,)),
        ],
        compiler_params=pltpu.CompilerParams(
            collective_id=0, has_side_effects=True, vmem_limit_bytes=63 * 1024 * 1024
        ),
        cost_estimate=pl.CostEstimate(flops=2_500_000_000, bytes_accessed=9_000_000, transcendentals=70_000),
        name="sage_layer",
    )(*inputs)


def finish_kernel(*refs):
    given, results, staged, in_sem, out_sem = refs[:5], refs[5:10], refs[10:15], refs[15], refs[16]
    reads = [pltpu.make_async_copy(given[k], staged[k], in_sem.at[k]) for k in range(5)]
    writes = [pltpu.make_async_copy(staged[k], results[k], out_sem.at[k]) for k in range(5)]
    for read in reads:
        read.start()
    for read, write in zip(reads, writes):
        read.wait()
        write.start()
    for write in writes:
        write.wait()


def finish(results):
    hbm = pl.BlockSpec(memory_space=pltpu.HBM)
    return pl.pallas_call(
        finish_kernel,
        out_shape=tuple(jax.ShapeDtypeStruct(x.shape, x.dtype) for x in results),
        in_specs=[hbm] * 5,
        out_specs=(hbm,) * 5,
        scratch_shapes=[
            *[pltpu.VMEM(x.shape, x.dtype) for x in results],
            pltpu.SemaphoreType.DMA((5,)),
            pltpu.SemaphoreType.DMA((5,)),
        ],
        compiler_params=pltpu.CompilerParams(vmem_limit_bytes=63 * 1024 * 1024),
        name="write_results",
    )(*results)


def shards(node_feats, tile_row, tile_col, tile_bits, w_self, w_neigh, bias, cotangent):
    rows_dev, width_in = node_feats.shape
    node_count = lax.axis_size("nodes")
    col_count = lax.axis_size("cols")
    per_dev = rows_dev // 128
    adj, deg = build(tile_row, tile_col, tile_bits, node_count * per_dev, col_count * per_dev)
    layer_out, feat_grad, self_grad, neigh_grad, bias_grad = finish(
        layer(adj, deg, node_feats, w_self, w_neigh, bias[None, :], cotangent, node_count, col_count)
    )
    return (layer_out, feat_grad, self_grad, neigh_grad, bias_grad[0])


def solution(mesh):
    return jax.shard_map(
        shards,
        mesh=mesh,
        in_specs=(
            P(("nodes", "cols"), None),
            P("nodes", "cols"),
            P("nodes", "cols"),
            P("nodes", "cols", None, None),
            P(),
            P(),
            P(),
            P(("nodes", "cols"), None),
        ),
        out_specs=(P(("nodes", "cols"), None), P(("nodes", "cols"), None), P(), P(), P()),
        check_vma=False,
    )
```

```python
import functools

import jax
import jax.numpy as jnp
from jax import lax
from jax.experimental import pallas as pl
from jax.experimental.pallas import tpu as pltpu
from jax.sharding import PartitionSpec as P


def build_kernel(row_ref, col_ref, bits_hbm, adj_hbm, deg_ref, count_ref, bits_ref, adj_ref, in_sem, out_sem):
    source_count, dest_count = count_ref.shape[:2]
    tile_count = bits_ref.shape[0]
    batch_count = in_sem.shape[0]
    batch = tile_count // batch_count

    def load(k):
        span = pl.ds(k * batch, batch)
        return pltpu.make_async_copy(bits_hbm.at[0, span], bits_ref.at[span], in_sem.at[k])

    for k in range(batch_count):
        load(k).start()
    zero = jnp.zeros((4, 16, 128), jnp.int32)

    def clear(s, _):
        for d in range(dest_count):
            count_ref[s, d] = zero
        return 0

    lax.fori_loop(0, source_count, clear, 0)

    def add_tile(t, _):
        r = row_ref[0, t]
        c = col_ref[0, t]
        word = bits_ref[t]
        spread = word | (word << 12)
        sums = [count_ref[c, r, j] + ((spread >> j) & 0x10001) for j in range(4)]
        for j in range(4):
            count_ref[c, r, j] = sums[j]
        return 0

    for k in range(batch_count):
        load(k).wait()
        lax.fori_loop(k * batch, (k + 1) * batch, add_tile, 0, unroll=4)

    deg_ref[...] = jnp.zeros_like(deg_ref)

    def store(s):
        span = pl.ds(pl.multiple_of(s * 128, 128), 128)
        return pltpu.make_async_copy(adj_ref.at[span], adj_hbm.at[span], out_sem.at[s])

    def expand(s, _):
        for d in range(dest_count):
            lanes = slice(d * 128, (d + 1) * 128)
            total = jnp.zeros((16, 128), jnp.float32)
            for j in range(4):
                pair = count_ref[s, d, j]
                low = (pair & 0xFFFF).astype(jnp.float32)
                high = (pair >> 16).astype(jnp.float32)
                total = total + (low + high)
                adj_ref[pl.ds(s * 128 + j * 16, 16), lanes] = low.astype(jnp.bfloat16)
                adj_ref[pl.ds(s * 128 + (j + 4) * 16, 16), lanes] = high.astype(jnp.bfloat16)
            deg_ref[:, lanes] += total
        store(s).start()
        return 0

    lax.fori_loop(0, source_count, expand, 0)
    for s in range(source_count):
        store(s).wait()


def build(tile_row, tile_col, tile_bits, source_count, dest_count):
    smem = pl.BlockSpec(memory_space=pltpu.SMEM)
    hbm = pl.BlockSpec(memory_space=pltpu.HBM)
    tile_count = tile_row.shape[1]
    batch_count = 4 if tile_count % 16 == 0 else 1
    adj_shape = (source_count * 128, dest_count * 128)
    return pl.pallas_call(
        build_kernel,
        out_shape=(
            jax.ShapeDtypeStruct(adj_shape, jnp.bfloat16),
            jax.ShapeDtypeStruct((16, dest_count * 128), jnp.float32),
        ),
        in_specs=[smem, smem, hbm],
        out_specs=(hbm, pl.BlockSpec(memory_space=pltpu.VMEM)),
        scratch_shapes=[
            pltpu.VMEM((source_count, dest_count, 4, 16, 128), jnp.int32),
            pltpu.VMEM((tile_count, 16, 128), jnp.int32),
            pltpu.VMEM(adj_shape, jnp.bfloat16),
            pltpu.SemaphoreType.DMA((batch_count,)),
            pltpu.SemaphoreType.DMA((source_count,)),
        ],
        compiler_params=pltpu.CompilerParams(vmem_limit_bytes=63 * 1024 * 1024),
        cost_estimate=pl.CostEstimate(flops=20_000_000, bytes_accessed=8_000_000, transcendentals=0),
        name="build_adjacency",
    )(tile_row, tile_col, tile_bits)


def transposed(block):
    return block.astype(jnp.float32).T.astype(block.dtype)


def dot(left, right):
    return jnp.dot(left, right, preferred_element_type=jnp.float32)


def dot_nt(left, right):
    return lax.dot_general(left, right, (((1,), (1,)), ((), ())), preferred_element_type=jnp.float32)


def layer_kernel(node_count, col_count, piece, *refs):
    hbm_in, outs, scratch = refs[:7], refs[7:12], refs[12:]
    (layer_out, feat_grad, self_grad, neigh_grad, bias_grad) = outs
    local, load_sem = scratch[:7], scratch[7]
    (adj, deg, feats, w_self, w_neigh, bias, cot) = local
    (blocks, acc, own_source, sib_out, sib_in, sum_out, sum_in, mean_all, src_out, src_in, comb_out, comb_in, part_out, part_in,
     node_out, node_in, full, up_send, down_send, across_send, block_recv, sib_send, sib_recv, sum_send, sum_recv,
     mean_send, mean_recv, pass_send, src_send, src_recv, comb_send, comb_recv, part_send, part_recv,
     node_send, node_recv, piece_send, piece_recv, full_send, full_recv) = scratch[8:]
    n = lax.axis_index("nodes")
    c = lax.axis_index("cols")
    rows = feats.shape[0]
    width = feats.shape[1]
    f32, bf16 = jnp.float32, jnp.bfloat16
    length = node_count // 2
    place = lax.div(n, 2)
    side = lax.rem(n, 2)
    partner = place * 2 + 1 - side

    def load(k):
        return pltpu.make_async_copy(hbm_in[k], local[k], load_sem.at[k])

    for k in (2, 0, 1, 3, 4, 5, 6):
        load(k).start()

    def node_at(i):
        return lax.rem(n + i, node_count)

    def col_at(i):
        return lax.rem(c + i, col_count)

    def block(k):
        return pl.ds(pl.multiple_of(k * rows, rows), rows)

    def to_col(src, dst, send, recv, i):
        return pltpu.make_async_remote_copy(
            src_ref=src, dst_ref=dst, send_sem=send, recv_sem=recv,
            device_id=(n, col_at(i)), device_id_type=pl.DeviceIdType.MESH)

    def to_node(src, dst, send, recv, i):
        return pltpu.make_async_remote_copy(
            src_ref=src, dst_ref=dst, send_sem=send, recv_sem=recv,
            device_id=(node_at(i), c), device_id_type=pl.DeviceIdType.MESH)

    pairs = col_count // 2
    core = lax.rem(c, 2)
    line = lax.div(c, 2)

    def col_of(i, k):
        return lax.rem(line + i, pairs) * 2 + k

    def to_sibling(src, dst, send, recv):
        return pltpu.make_async_remote_copy(
            src_ref=src, dst_ref=dst, send_sem=send, recv_sem=recv,
            device_id=(n, line * 2 + 1 - core), device_id_type=pl.DeviceIdType.MESH)

    def to_peer(src, dst, send, recv, i):
        return pltpu.make_async_remote_copy(
            src_ref=src, dst_ref=dst, send_sem=send, recv_sem=recv,
            device_id=(n, col_of(i, core)), device_id_type=pl.DeviceIdType.MESH)

    def to_device(src, dst, send, recv, node):
        return pltpu.make_async_remote_copy(
            src_ref=src, dst_ref=dst, send_sem=send, recv_sem=recv,
            device_id=(node, c), device_id_type=pl.DeviceIdType.MESH)

    barrier = pltpu.get_barrier_semaphore()
    for i in range(1, col_count):
        pl.semaphore_signal(barrier, inc=1, device_id=(n, col_at(i)), device_id_type=pl.DeviceIdType.MESH)
    for i in range(1, node_count):
        pl.semaphore_signal(barrier, inc=1, device_id=(node_at(i), c), device_id_type=pl.DeviceIdType.MESH)
    pl.semaphore_wait(barrier, col_count + node_count - 2)

    to = lax.broadcasted_iota(jnp.int32, (rows, rows), 0)
    frm = lax.broadcasted_iota(jnp.int32, (rows, rows), 1)
    want = (to // 128) * 128 + (to % 8) * 16 + (to % 128) // 8
    order = jnp.where(frm == want, 1.0, 0.0).astype(bf16)

    def up(b):
        return to_device(blocks.at[b], blocks.at[b], up_send.at[b], block_recv.at[b], n + 2)

    def down(b):
        return to_device(blocks.at[b], blocks.at[b], down_send.at[b], block_recv.at[b], n - 2)

    def across(b):
        return to_device(blocks.at[b], blocks.at[b], across_send.at[b], block_recv.at[b], partner)

    def accumulate(b):
        acc[...] += dot(blocks[b], adj[block(b), :])

    load(2).wait()
    feats_t = transposed(feats[...])
    blocks[n] = dot(feats_t, order).astype(bf16)

    @pl.when(place + 1 < length)
    def _():
        up(n).start()

    @pl.when(place > 0)
    def _():
        down(n).start()

    across(n).start()
    load(0).wait()
    acc[...] = dot(blocks[n], adj[block(n), :])

    def along(d, _):
        @pl.when(place - d >= 0)
        def _():
            b = n - 2 * d
            across(b).wait_recv()

            @pl.when(place + 1 < length)
            def _():
                up(b).start()

            across(b).start()

        @pl.when(place + d < length)
        def _():
            b = n + 2 * d
            across(b).wait_recv()

            @pl.when(place > 0)
            def _():
                down(b).start()

            across(b).start()

        @pl.when(place - d >= 0)
        def _():
            accumulate(n - 2 * d)

        @pl.when(place + d < length)
        def _():
            accumulate(n + 2 * d)

        return 0

    lax.fori_loop(1, length, along, 0)
    for k in (1, 3, 4, 5, 6):
        load(k).wait()
    self_act = dot(feats[...], w_self[...]) + bias[...]

    def opposite(d, _):
        @pl.when(place - d >= 0)
        def _():
            across(partner - 2 * d).wait_recv()
            accumulate(partner - 2 * d)

        @pl.when((place + d < length) & (d > 0))
        def _():
            across(partner + 2 * d).wait_recv()
            accumulate(partner + 2 * d)

        return 0

    lax.fori_loop(0, length, opposite, 0)

    def part_sum(col):
        return acc[:, block(col)]

    def part_degree(col):
        return jnp.sum(deg[:, block(col)], axis=0, keepdims=True)

    def sib_copy(i):
        return to_sibling(sib_out.at[i], sib_in.at[i], sib_send.at[i], sib_recv.at[i])

    def sum_copy(i):
        return to_peer(sum_out.at[i - 1], sum_in.at[i - 1], sum_send.at[i - 1], sum_recv.at[i - 1], i)

    digit = lax.broadcasted_iota(jnp.int32, (16, rows), 0)

    def pack(ref, slot, part, degree):
        high = jnp.floor(degree * (1.0 / 65536.0))
        rest = degree - high * 65536.0
        middle = jnp.floor(rest * (1.0 / 256.0))
        low = rest - middle * 256.0
        ref[slot, :width] = part.astype(bf16)
        ref[slot, width:] = jnp.where(digit == 0, high, jnp.where(digit == 1, middle, low)).astype(bf16)

    def unpack(ref, slot):
        tail = ref[slot, width:].astype(f32)
        return ref[slot, :width].astype(f32), tail[0:1] * 65536.0 + tail[1:2] * 256.0 + tail[2:3]

    for i in (*range(1, pairs), 0):
        col = col_of(i, 1 - core)
        pack(sib_out, i, part_sum(col), part_degree(col))
        sib_copy(i).start()
    for i in range(1, pairs):
        col = col_of(i, core)
        sib_copy(i).wait_recv()
        part, part_deg = unpack(sib_in, i)
        pack(sum_out, i - 1, part + part_sum(col), part_deg + part_degree(col))
        sum_copy(i).start()
    sib_copy(0).wait_recv()
    part, part_deg = unpack(sib_in, 0)
    summed = part + part_sum(c)
    degree = part_deg + part_degree(c)
    for i in range(1, pairs):
        sum_copy(i).wait_recv()
        part, part_deg = unpack(sum_in, i - 1)
        summed = summed + part
        degree = degree + part_deg
    degree = jnp.maximum(degree, 1.0)

    mean_t = summed / degree
    mean = mean_t.T.astype(bf16)
    mean_t = mean_t.astype(bf16)
    preact = self_act + dot(mean, w_neigh[...])
    gate = jax.nn.sigmoid(preact)
    layer_out[...] = (preact * gate).astype(bf16)
    pre_grad = (cot[...].astype(f32) * gate * (1.0 + preact * (1.0 - gate))).astype(bf16)
    mean_grad = dot_nt(w_neigh[...], pre_grad) / degree
    mean_all[block(c)] = mean_grad.T.astype(bf16)

    def mean_peer(i):
        held = mean_all.at[block(c)]
        return to_peer(held, held, mean_send.at[i - 1], mean_recv.at[c], i)

    def mean_sibling(i, k):
        held = mean_all.at[block(col_of(i, k))]
        return to_sibling(held, held, pass_send.at[i], mean_recv.at[col_of(i, k)])

    for i in range(1, pairs):
        mean_peer(i).start()
    mean_sibling(0, core).start()

    self_term = dot(feats_t, pre_grad)
    neigh_term = dot(mean_t, pre_grad)
    bias_term = jnp.sum(pre_grad.astype(f32), axis=0, keepdims=True)
    group = col_count * piece
    chunk = node_count * piece
    top = lax.broadcasted_iota(jnp.int32, (16, width), 0) == 0

    def split_bias(value):
        high = value.astype(bf16).astype(f32)
        return jnp.where(top, high, value - high).astype(bf16)

    def join_bias(value):
        pair = value.astype(f32)
        return pair[0:1] + pair[1:2]

    terms = jnp.concatenate([self_term, neigh_term], axis=0)
    spare = node_count * group - 2 * width
    if spare:
        terms = jnp.concatenate([terms, jnp.zeros((spare, width), f32)], axis=0)
    for k in range(node_count):
        node_out[k, :group] = terms[k * group : (k + 1) * group].astype(bf16)
        node_out[k, group:] = split_bias(bias_term)

    def node_copy(i):
        return to_node(node_out.at[node_at(i)], node_in.at[i - 1], node_send.at[i - 1], node_recv.at[i - 1], i)

    for i in range(1, node_count):
        node_copy(i).start()

    self_feat = dot_nt(pre_grad, w_self[...])
    for i in range(1, pairs):
        mean_sibling(i, core).wait_recv()
        mean_sibling(i, core).start()
    for i in range(pairs):
        mean_sibling(i, 1 - core).wait_recv()

    def source_part(node):
        return dot(adj[block(node), :], mean_all[...])

    def goal(i):
        return jnp.where(place * 2 < length, length - 1 - i, i)

    def src_copy(i):
        return to_device(src_out.at[i], src_in.at[i], src_send.at[i], src_recv.at[i], partner)

    def comb_copy(i, sender):
        return to_device(comb_out.at[i], comb_in.at[sender], comb_send.at[i], comb_recv.at[sender], goal(i) * 2 + side)

    def send_source(i, _):
        src_out[i] = source_part(goal(i) * 2 + 1 - side).astype(bf16)
        src_copy(i).start()
        return 0

    lax.fori_loop(0, length, send_source, 0)

    total = node_out[n, :group].astype(f32)
    bias_total = bias_term
    for i in range(1, node_count):
        node_copy(i).wait_recv()
        total = total + node_in[i - 1, :group].astype(f32)
        bias_total = bias_total + join_bias(node_in[i - 1, group:])
    for k in range(col_count):
        part_out[k, :piece] = total[k * piece : (k + 1) * piece].astype(bf16)
        part_out[k, piece:] = split_bias(bias_total)

    def part_copy(i):
        return to_col(part_out.at[col_at(i)], part_in.at[i - 1], part_send.at[i - 1], part_recv.at[i - 1], i)

    for i in range(1, col_count):
        part_copy(i).start()

    def combine(i, _):
        part = source_part(goal(i) * 2 + side)
        src_copy(i).wait_recv()
        part = part + src_in[i].astype(f32)

        @pl.when(goal(i) != place)
        def _():
            comb_out[i] = part.astype(bf16)
            comb_copy(i, place).start()

        @pl.when(goal(i) == place)
        def _():
            own_source[...] = part

        return 0

    lax.fori_loop(0, 1, combine, 0)
    mine = part_out[c, :piece].astype(f32)
    for i in range(1, col_count):
        part_copy(i).wait_recv()
        mine = mine + part_in[i - 1, :piece].astype(f32)
        bias_total = bias_total + join_bias(part_in[i - 1, piece:])
    bias_grad[...] = bias_total

    own_rows = pl.ds(pl.multiple_of(n * piece, piece), piece)
    full[c, own_rows] = mine.astype(bf16)

    def piece_copy(i):
        return to_node(full.at[c, own_rows], full.at[c, own_rows], piece_send.at[i - 1], piece_recv.at[i - 1], i)

    for i in range(1, node_count):
        piece_copy(i).start()
    lax.fori_loop(1, length, combine, 0)
    for i in range(1, node_count):
        piece_copy(i).wait_recv()

    def full_copy(i):
        return to_col(full.at[c], full.at[c], full_send.at[i - 1], full_recv.at[i - 1], i)

    for i in range(1, col_count):
        full_copy(i).start()

    def collect(j, _):
        @pl.when(j != place)
        def _():
            comb_copy(0, j).wait_recv()
            own_source[...] += comb_in[j].astype(f32)

        return 0

    lax.fori_loop(0, length, collect, 0)
    source = own_source[...]
    high = source.astype(bf16)
    low = (source - high.astype(f32)).astype(bf16)
    feat_grad[...] = (self_feat + (dot(order, high) + dot(order, low))).astype(bf16)

    for i in range(1, col_count):
        full_copy(i).wait_recv()
    for k in range(col_count):
        for part in range(chunk // piece):
            row = (part * col_count + k) * piece
            if row < width:
                self_grad[row : row + piece] = full[k, part * piece : (part + 1) * piece].astype(f32)
            elif row < 2 * width:
                neigh_grad[row - width : row - width + piece] = full[
                    k, part * piece : (part + 1) * piece
                ].astype(f32)
    for i in range(1, col_count):
        part_copy(i).wait_send()
        full_copy(i).wait_send()

    for i in range(1, pairs):
        sum_copy(i).wait_send()
        mean_peer(i).wait_send()
    for i in range(pairs):
        sib_copy(i).wait_send()
        mean_sibling(i, core).wait_send()

    def drain(i, _):
        src_copy(i).wait_send()
        across(i * 2 + side).wait_send()

        @pl.when(goal(i) != place)
        def _():
            comb_copy(i, place).wait_send()

        @pl.when((i <= place) & (place + 1 < length))
        def _():
            up(i * 2 + side).wait_send()

        @pl.when((i >= place) & (place > 0))
        def _():
            down(i * 2 + side).wait_send()

        return 0

    lax.fori_loop(0, length, drain, 0)
    for i in range(1, node_count):
        node_copy(i).wait_send()
        piece_copy(i).wait_send()


def layer(adj, deg, feats, w_self, w_neigh, bias, cot, node_count, col_count):
    rows, width = feats.shape
    piece = max(16, 2 * width // (node_count * col_count))
    group = col_count * piece
    chunk = node_count * piece
    vmem = pl.BlockSpec(memory_space=pltpu.VMEM)
    hbm = pl.BlockSpec(memory_space=pltpu.HBM)
    inputs = (adj, deg, feats, w_self, w_neigh, bias, cot)
    length = node_count // 2
    pairs = col_count // 2
    bf16, f32 = jnp.bfloat16, jnp.float32
    others, peers = col_count - 1, node_count - 1
    sems = pltpu.SemaphoreType.DMA
    return pl.pallas_call(
        functools.partial(layer_kernel, node_count, col_count, piece),
        out_shape=(
            jax.ShapeDtypeStruct((rows, width), bf16),
            jax.ShapeDtypeStruct((rows, width), bf16),
            jax.ShapeDtypeStruct((width, width), f32),
            jax.ShapeDtypeStruct((width, width), f32),
            jax.ShapeDtypeStruct((1, width), f32),
        ),
        in_specs=[hbm] * 7,
        out_specs=(vmem,) * 5,
        scratch_shapes=[
            *[pltpu.VMEM(x.shape, x.dtype) for x in inputs],
            sems((7,)),
            pltpu.VMEM((node_count, width, rows), bf16),
            pltpu.VMEM((width, col_count * rows), f32),
            pltpu.VMEM((rows, width), f32),
            pltpu.VMEM((pairs, width + 16, rows), bf16),
            pltpu.VMEM((pairs, width + 16, rows), bf16),
            pltpu.VMEM((pairs - 1, width + 16, rows), bf16),
            pltpu.VMEM((pairs - 1, width + 16, rows), bf16),
            pltpu.VMEM((col_count * rows, width), bf16),
            pltpu.VMEM((length, rows, width), bf16),
            pltpu.VMEM((length, rows, width), bf16),
            pltpu.VMEM((length, rows, width), bf16),
            pltpu.VMEM((length, rows, width), bf16),
            pltpu.VMEM((col_count, piece + 16, width), bf16),
            pltpu.VMEM((others, piece + 16, width), bf16),
            pltpu.VMEM((node_count, group + 16, width), bf16),
            pltpu.VMEM((peers, group + 16, width), bf16),
            pltpu.VMEM((col_count, chunk, width), bf16),
            sems((node_count,)), sems((node_count,)), sems((node_count,)), sems((node_count,)),
            sems((pairs,)), sems((pairs,)), sems((pairs - 1,)), sems((pairs - 1,)),
            sems((pairs - 1,)), sems((col_count,)), sems((pairs,)),
            sems((length,)), sems((length,)), sems((length,)), sems((length,)),
            sems((others,)), sems((others,)),
            sems((peers,)), sems((peers,)), sems((peers,)), sems((peers,)),
            sems((others,)), sems((others,)),
        ],
        compiler_params=pltpu.CompilerParams(
            collective_id=0, has_side_effects=True, vmem_limit_bytes=63 * 1024 * 1024
        ),
        cost_estimate=pl.CostEstimate(flops=2_500_000_000, bytes_accessed=9_000_000, transcendentals=70_000),
        name="sage_layer",
    )(*inputs)


def finish_kernel(*refs):
    given, results, staged, in_sem, out_sem = refs[:5], refs[5:10], refs[10:15], refs[15], refs[16]
    reads = [pltpu.make_async_copy(given[k], staged[k], in_sem.at[k]) for k in range(5)]
    writes = [pltpu.make_async_copy(staged[k], results[k], out_sem.at[k]) for k in range(5)]
    for read in reads:
        read.start()
    for read, write in zip(reads, writes):
        read.wait()
        write.start()
    for write in writes:
        write.wait()


def finish(results):
    hbm = pl.BlockSpec(memory_space=pltpu.HBM)
    return pl.pallas_call(
        finish_kernel,
        out_shape=tuple(jax.ShapeDtypeStruct(x.shape, x.dtype) for x in results),
        in_specs=[hbm] * 5,
        out_specs=(hbm,) * 5,
        scratch_shapes=[
            *[pltpu.VMEM(x.shape, x.dtype) for x in results],
            pltpu.SemaphoreType.DMA((5,)),
            pltpu.SemaphoreType.DMA((5,)),
        ],
        compiler_params=pltpu.CompilerParams(vmem_limit_bytes=63 * 1024 * 1024),
        name="write_results",
    )(*results)


def shards(node_feats, tile_row, tile_col, tile_bits, w_self, w_neigh, bias, cotangent):
    rows_dev, width_in = node_feats.shape
    node_count = lax.axis_size("nodes")
    col_count = lax.axis_size("cols")
    per_dev = rows_dev // 128
    adj, deg = build(tile_row, tile_col, tile_bits, node_count * per_dev, col_count * per_dev)
    layer_out, feat_grad, self_grad, neigh_grad, bias_grad = finish(
        layer(adj, deg, node_feats, w_self, w_neigh, bias[None, :], cotangent, node_count, col_count)
    )
    return (layer_out, feat_grad, self_grad, neigh_grad, bias_grad[0])


def solution(mesh):
    return jax.shard_map(
        shards,
        mesh=mesh,
        in_specs=(
            P(("nodes", "cols"), None),
            P("nodes", "cols"),
            P("nodes", "cols"),
            P("nodes", "cols", None, None),
            P(),
            P(),
            P(),
            P(("nodes", "cols"), None),
        ),
        out_specs=(P(("nodes", "cols"), None), P(("nodes", "cols"), None), P(), P(), P()),
        check_vma=False,
    )
```

```python
import functools

import jax
import jax.numpy as jnp
from jax import lax
from jax.experimental import pallas as pl
from jax.experimental.pallas import tpu as pltpu
from jax.sharding import PartitionSpec as P


def build_kernel(row_ref, col_ref, bits_hbm, adj_hbm, deg_ref, count_ref, other_ref, bits_ref, adj_ref, in_sem, out_sem):
    source_count, dest_count = count_ref.shape[:2]
    tile_count = bits_ref.shape[0]
    batch_count = in_sem.shape[0]
    batch = tile_count // batch_count

    def load(k):
        span = pl.ds(k * batch, batch)
        return pltpu.make_async_copy(bits_hbm.at[0, span], bits_ref.at[span], in_sem.at[k])

    for k in range(batch_count):
        load(k).start()
    zero = jnp.zeros((4, 16, 128), jnp.int32)

    def clear(s, _):
        for d in range(dest_count):
            count_ref[s, d] = zero
            other_ref[s, d] = zero
        return 0

    lax.fori_loop(0, source_count, clear, 0)

    half = batch // 2

    def add_tiles(t, _):
        pending = []
        for counts, at in ((count_ref, t), (other_ref, t + half)):
            r = row_ref[0, at]
            c = col_ref[0, at]
            word = bits_ref[at]
            spread = word | (word << 12)
            pending.append((counts, r, c, [counts[c, r, j] + ((spread >> j) & 0x10001) for j in range(4)]))
        for counts, r, c, sums in pending:
            for j in range(4):
                counts[c, r, j] = sums[j]
        return 0

    for k in range(batch_count):
        load(k).wait()
        lax.fori_loop(k * batch, k * batch + half, add_tiles, 0, unroll=4)

    deg_ref[...] = jnp.zeros_like(deg_ref)

    def store(s):
        span = pl.ds(pl.multiple_of(s * 128, 128), 128)
        return pltpu.make_async_copy(adj_ref.at[span], adj_hbm.at[span], out_sem.at[s])

    def expand(s, _):
        for d in range(dest_count):
            lanes = slice(d * 128, (d + 1) * 128)
            total = jnp.zeros((16, 128), jnp.float32)
            for j in range(4):
                pair = count_ref[s, d, j] + other_ref[s, d, j]
                low = (pair & 0xFFFF).astype(jnp.float32)
                high = (pair >> 16).astype(jnp.float32)
                total = total + (low + high)
                adj_ref[pl.ds(s * 128 + j * 16, 16), lanes] = low.astype(jnp.bfloat16)
                adj_ref[pl.ds(s * 128 + (j + 4) * 16, 16), lanes] = high.astype(jnp.bfloat16)
            deg_ref[:, lanes] += total
        store(s).start()
        return 0

    lax.fori_loop(0, source_count, expand, 0)
    for s in range(source_count):
        store(s).wait()


def build(tile_row, tile_col, tile_bits, source_count, dest_count):
    smem = pl.BlockSpec(memory_space=pltpu.SMEM)
    hbm = pl.BlockSpec(memory_space=pltpu.HBM)
    tile_count = tile_row.shape[1]
    batch_count = 4 if tile_count % 16 == 0 else 1
    adj_shape = (source_count * 128, dest_count * 128)
    return pl.pallas_call(
        build_kernel,
        out_shape=(
            jax.ShapeDtypeStruct(adj_shape, jnp.bfloat16),
            jax.ShapeDtypeStruct((16, dest_count * 128), jnp.float32),
        ),
        in_specs=[smem, smem, hbm],
        out_specs=(hbm, pl.BlockSpec(memory_space=pltpu.VMEM)),
        scratch_shapes=[
            pltpu.VMEM((source_count, dest_count, 4, 16, 128), jnp.int32),
            pltpu.VMEM((source_count, dest_count, 4, 16, 128), jnp.int32),
            pltpu.VMEM((tile_count, 16, 128), jnp.int32),
            pltpu.VMEM(adj_shape, jnp.bfloat16),
            pltpu.SemaphoreType.DMA((batch_count,)),
            pltpu.SemaphoreType.DMA((source_count,)),
        ],
        compiler_params=pltpu.CompilerParams(vmem_limit_bytes=63 * 1024 * 1024),
        cost_estimate=pl.CostEstimate(flops=20_000_000, bytes_accessed=8_000_000, transcendentals=0),
        name="build_adjacency",
    )(tile_row, tile_col, tile_bits)


def transposed(block):
    return block.astype(jnp.float32).T.astype(block.dtype)


def dot(left, right):
    return jnp.dot(left, right, preferred_element_type=jnp.float32)


def dot_nt(left, right):
    return lax.dot_general(left, right, (((1,), (1,)), ((), ())), preferred_element_type=jnp.float32)


def layer_kernel(node_count, col_count, piece, *refs):
    hbm_in, outs, scratch = refs[:7], refs[7:12], refs[12:]
    (layer_out, feat_grad, self_grad, neigh_grad, bias_grad) = outs
    local, load_sem = scratch[:7], scratch[7]
    (adj, deg, feats, w_self, w_neigh, bias, cot) = local
    (blocks, acc, own_source, sib_out, sib_in, sum_out, sum_in, mean_all, src_out, src_in, comb_out, comb_in, part_out, part_in,
     node_out, node_in, full, up_send, down_send, across_send, block_recv, sib_send, sib_recv, sum_send, sum_recv,
     mean_send, mean_recv, pass_send, src_send, src_recv, comb_send, comb_recv, part_send, part_recv,
     node_send, node_recv, piece_send, piece_recv, full_send, full_recv) = scratch[8:]
    n = lax.axis_index("nodes")
    c = lax.axis_index("cols")
    rows = feats.shape[0]
    width = feats.shape[1]
    f32, bf16 = jnp.float32, jnp.bfloat16
    length = node_count // 2
    place = lax.div(n, 2)
    side = lax.rem(n, 2)
    partner = place * 2 + 1 - side

    def load(k):
        return pltpu.make_async_copy(hbm_in[k], local[k], load_sem.at[k])

    for k in (2, 0, 1, 3, 4, 5, 6):
        load(k).start()

    def node_at(i):
        return lax.rem(n + i, node_count)

    def col_at(i):
        return lax.rem(c + i, col_count)

    def block(k):
        return pl.ds(pl.multiple_of(k * rows, rows), rows)

    def to_col(src, dst, send, recv, i):
        return pltpu.make_async_remote_copy(
            src_ref=src, dst_ref=dst, send_sem=send, recv_sem=recv,
            device_id=(n, col_at(i)), device_id_type=pl.DeviceIdType.MESH)

    def to_node(src, dst, send, recv, i):
        return pltpu.make_async_remote_copy(
            src_ref=src, dst_ref=dst, send_sem=send, recv_sem=recv,
            device_id=(node_at(i), c), device_id_type=pl.DeviceIdType.MESH)

    pairs = col_count // 2
    core = lax.rem(c, 2)
    line = lax.div(c, 2)

    def col_of(i, k):
        return lax.rem(line + i, pairs) * 2 + k

    def to_sibling(src, dst, send, recv):
        return pltpu.make_async_remote_copy(
            src_ref=src, dst_ref=dst, send_sem=send, recv_sem=recv,
            device_id=(n, line * 2 + 1 - core), device_id_type=pl.DeviceIdType.MESH)

    def to_peer(src, dst, send, recv, i):
        return pltpu.make_async_remote_copy(
            src_ref=src, dst_ref=dst, send_sem=send, recv_sem=recv,
            device_id=(n, col_of(i, core)), device_id_type=pl.DeviceIdType.MESH)

    def to_device(src, dst, send, recv, node):
        return pltpu.make_async_remote_copy(
            src_ref=src, dst_ref=dst, send_sem=send, recv_sem=recv,
            device_id=(node, c), device_id_type=pl.DeviceIdType.MESH)

    barrier = pltpu.get_barrier_semaphore()
    for i in range(1, col_count):
        pl.semaphore_signal(barrier, inc=1, device_id=(n, col_at(i)), device_id_type=pl.DeviceIdType.MESH)
    for i in range(1, node_count):
        pl.semaphore_signal(barrier, inc=1, device_id=(node_at(i), c), device_id_type=pl.DeviceIdType.MESH)
    pl.semaphore_wait(barrier, col_count + node_count - 2)

    to = lax.broadcasted_iota(jnp.int32, (rows, rows), 0)
    frm = lax.broadcasted_iota(jnp.int32, (rows, rows), 1)
    want = (to // 128) * 128 + (to % 8) * 16 + (to % 128) // 8
    order = jnp.where(frm == want, 1.0, 0.0).astype(bf16)

    def up(b):
        return to_device(blocks.at[b], blocks.at[b], up_send.at[b], block_recv.at[b], n + 2)

    def down(b):
        return to_device(blocks.at[b], blocks.at[b], down_send.at[b], block_recv.at[b], n - 2)

    def across(b):
        return to_device(blocks.at[b], blocks.at[b], across_send.at[b], block_recv.at[b], partner)

    def accumulate(b):
        acc[...] += dot(blocks[b], adj[block(b), :])

    load(2).wait()
    feats_t = transposed(feats[...])
    blocks[n] = dot(feats_t, order).astype(bf16)

    @pl.when(place + 1 < length)
    def _():
        up(n).start()

    @pl.when(place > 0)
    def _():
        down(n).start()

    across(n).start()
    load(0).wait()
    acc[...] = dot(blocks[n], adj[block(n), :])

    def along(d, _):
        @pl.when(place - d >= 0)
        def _():
            b = n - 2 * d
            across(b).wait_recv()

            @pl.when(place + 1 < length)
            def _():
                up(b).start()

            across(b).start()

        @pl.when(place + d < length)
        def _():
            b = n + 2 * d
            across(b).wait_recv()

            @pl.when(place > 0)
            def _():
                down(b).start()

            across(b).start()

        @pl.when(place - d >= 0)
        def _():
            accumulate(n - 2 * d)

        @pl.when(place + d < length)
        def _():
            accumulate(n + 2 * d)

        return 0

    lax.fori_loop(1, length, along, 0)
    for k in (1, 3, 4, 5, 6):
        load(k).wait()
    self_act = dot(feats[...], w_self[...]) + bias[...]

    def opposite(d, _):
        @pl.when(place - d >= 0)
        def _():
            across(partner - 2 * d).wait_recv()
            accumulate(partner - 2 * d)

        @pl.when((place + d < length) & (d > 0))
        def _():
            across(partner + 2 * d).wait_recv()
            accumulate(partner + 2 * d)

        return 0

    lax.fori_loop(0, length, opposite, 0)

    def part_sum(col):
        return acc[:, block(col)]

    def part_degree(col):
        return jnp.sum(deg[:, block(col)], axis=0, keepdims=True)

    def sib_copy(i):
        return to_sibling(sib_out.at[i], sib_in.at[i], sib_send.at[i], sib_recv.at[i])

    def sum_copy(i):
        return to_peer(sum_out.at[i - 1], sum_in.at[i - 1], sum_send.at[i - 1], sum_recv.at[i - 1], i)

    digit = lax.broadcasted_iota(jnp.int32, (16, rows), 0)

    def pack(ref, slot, part, degree):
        high = jnp.floor(degree * (1.0 / 65536.0))
        rest = degree - high * 65536.0
        middle = jnp.floor(rest * (1.0 / 256.0))
        low = rest - middle * 256.0
        ref[slot, :width] = part.astype(bf16)
        ref[slot, width:] = jnp.where(digit == 0, high, jnp.where(digit == 1, middle, low)).astype(bf16)

    def unpack(ref, slot):
        tail = ref[slot, width:].astype(f32)
        return ref[slot, :width].astype(f32), tail[0:1] * 65536.0 + tail[1:2] * 256.0 + tail[2:3]

    for i in (*range(1, pairs), 0):
        col = col_of(i, 1 - core)
        pack(sib_out, i, part_sum(col), part_degree(col))
        sib_copy(i).start()
    for i in range(1, pairs):
        col = col_of(i, core)
        sib_copy(i).wait_recv()
        part, part_deg = unpack(sib_in, i)
        pack(sum_out, i - 1, part + part_sum(col), part_deg + part_degree(col))
        sum_copy(i).start()
    sib_copy(0).wait_recv()
    part, part_deg = unpack(sib_in, 0)
    summed = part + part_sum(c)
    degree = part_deg + part_degree(c)
    for i in range(1, pairs):
        sum_copy(i).wait_recv()
        part, part_deg = unpack(sum_in, i - 1)
        summed = summed + part
        degree = degree + part_deg
    degree = jnp.maximum(degree, 1.0)

    mean_t = summed / degree
    mean = mean_t.T.astype(bf16)
    mean_t = mean_t.astype(bf16)
    preact = self_act + dot(mean, w_neigh[...])
    gate = jax.nn.sigmoid(preact)
    layer_out[...] = (preact * gate).astype(bf16)
    pre_grad = (cot[...].astype(f32) * gate * (1.0 + preact * (1.0 - gate))).astype(bf16)
    mean_grad = dot_nt(w_neigh[...], pre_grad) / degree
    mean_all[block(c)] = mean_grad.T.astype(bf16)

    def mean_peer(i):
        held = mean_all.at[block(c)]
        return to_peer(held, held, mean_send.at[i - 1], mean_recv.at[c], i)

    def mean_sibling(i, k):
        held = mean_all.at[block(col_of(i, k))]
        return to_sibling(held, held, pass_send.at[i], mean_recv.at[col_of(i, k)])

    for i in range(1, pairs):
        mean_peer(i).start()
    mean_sibling(0, core).start()

    self_term = dot(feats_t, pre_grad)
    neigh_term = dot(mean_t, pre_grad)
    bias_term = jnp.sum(pre_grad.astype(f32), axis=0, keepdims=True)
    group = col_count * piece
    chunk = node_count * piece
    top = lax.broadcasted_iota(jnp.int32, (16, width), 0) == 0

    def split_bias(value):
        high = value.astype(bf16).astype(f32)
        return jnp.where(top, high, value - high).astype(bf16)

    def join_bias(value):
        pair = value.astype(f32)
        return pair[0:1] + pair[1:2]

    terms = jnp.concatenate([self_term, neigh_term], axis=0)
    spare = node_count * group - 2 * width
    if spare:
        terms = jnp.concatenate([terms, jnp.zeros((spare, width), f32)], axis=0)
    for k in range(node_count):
        node_out[k, :group] = terms[k * group : (k + 1) * group].astype(bf16)
        node_out[k, group:] = split_bias(bias_term)

    def node_copy(i):
        return to_node(node_out.at[node_at(i)], node_in.at[i - 1], node_send.at[i - 1], node_recv.at[i - 1], i)

    for i in range(1, node_count):
        node_copy(i).start()

    self_feat = dot_nt(pre_grad, w_self[...])
    for i in range(1, pairs):
        mean_sibling(i, core).wait_recv()
        mean_sibling(i, core).start()
    for i in range(pairs):
        mean_sibling(i, 1 - core).wait_recv()

    def source_part(node):
        return dot(adj[block(node), :], mean_all[...])

    def goal(i):
        return jnp.where(place * 2 < length, length - 1 - i, i)

    def src_copy(i):
        return to_device(src_out.at[i], src_in.at[i], src_send.at[i], src_recv.at[i], partner)

    def comb_copy(i, sender):
        return to_device(comb_out.at[i], comb_in.at[sender], comb_send.at[i], comb_recv.at[sender], goal(i) * 2 + side)

    def send_source(i, _):
        src_out[i] = source_part(goal(i) * 2 + 1 - side).astype(bf16)
        src_copy(i).start()
        return 0

    lax.fori_loop(0, length, send_source, 0)

    def combine(i, _):
        part = source_part(goal(i) * 2 + side)
        src_copy(i).wait_recv()
        part = part + src_in[i].astype(f32)

        @pl.when(goal(i) != place)
        def _():
            comb_out[i] = part.astype(bf16)
            comb_copy(i, place).start()

        @pl.when(goal(i) == place)
        def _():
            own_source[...] = part

        return 0

    lax.fori_loop(0, 1, combine, 0)
    total = node_out[n, :group].astype(f32)
    bias_total = bias_term
    for i in range(1, node_count):
        node_copy(i).wait_recv()
        total = total + node_in[i - 1, :group].astype(f32)
        bias_total = bias_total + join_bias(node_in[i - 1, group:])
    for k in range(col_count):
        part_out[k, :piece] = total[k * piece : (k + 1) * piece].astype(bf16)
        part_out[k, piece:] = split_bias(bias_total)

    def part_copy(i):
        return to_col(part_out.at[col_at(i)], part_in.at[i - 1], part_send.at[i - 1], part_recv.at[i - 1], i)

    for i in range(1, col_count):
        part_copy(i).start()

    lax.fori_loop(1, 2, combine, 0)
    mine = part_out[c, :piece].astype(f32)
    for i in range(1, col_count):
        part_copy(i).wait_recv()
        mine = mine + part_in[i - 1, :piece].astype(f32)
        bias_total = bias_total + join_bias(part_in[i - 1, piece:])
    bias_grad[...] = bias_total

    own_rows = pl.ds(pl.multiple_of(n * piece, piece), piece)
    full[c, own_rows] = mine.astype(bf16)

    def piece_copy(i):
        return to_node(full.at[c, own_rows], full.at[c, own_rows], piece_send.at[i - 1], piece_recv.at[i - 1], i)

    for i in range(1, node_count):
        piece_copy(i).start()
    lax.fori_loop(2, length, combine, 0)
    for i in range(1, node_count):
        piece_copy(i).wait_recv()

    def full_copy(i):
        return to_col(full.at[c], full.at[c], full_send.at[i - 1], full_recv.at[i - 1], i)

    for i in range(1, col_count):
        full_copy(i).start()

    def collect(j, _):
        @pl.when(j != place)
        def _():
            comb_copy(0, j).wait_recv()
            own_source[...] += comb_in[j].astype(f32)

        return 0

    lax.fori_loop(0, length, collect, 0)
    source = own_source[...]
    high = source.astype(bf16)
    low = (source - high.astype(f32)).astype(bf16)
    feat_grad[...] = (self_feat + (dot(order, high) + dot(order, low))).astype(bf16)

    for i in range(1, col_count):
        full_copy(i).wait_recv()
    for k in range(col_count):
        for part in range(chunk // piece):
            row = (part * col_count + k) * piece
            if row < width:
                self_grad[row : row + piece] = full[k, part * piece : (part + 1) * piece].astype(f32)
            elif row < 2 * width:
                neigh_grad[row - width : row - width + piece] = full[
                    k, part * piece : (part + 1) * piece
                ].astype(f32)
    for i in range(1, col_count):
        part_copy(i).wait_send()
        full_copy(i).wait_send()

    for i in range(1, pairs):
        sum_copy(i).wait_send()
        mean_peer(i).wait_send()
    for i in range(pairs):
        sib_copy(i).wait_send()
        mean_sibling(i, core).wait_send()

    def drain(i, _):
        src_copy(i).wait_send()
        across(i * 2 + side).wait_send()

        @pl.when(goal(i) != place)
        def _():
            comb_copy(i, place).wait_send()

        @pl.when((i <= place) & (place + 1 < length))
        def _():
            up(i * 2 + side).wait_send()

        @pl.when((i >= place) & (place > 0))
        def _():
            down(i * 2 + side).wait_send()

        return 0

    lax.fori_loop(0, length, drain, 0)
    for i in range(1, node_count):
        node_copy(i).wait_send()
        piece_copy(i).wait_send()


def layer(adj, deg, feats, w_self, w_neigh, bias, cot, node_count, col_count):
    rows, width = feats.shape
    piece = max(16, 2 * width // (node_count * col_count))
    group = col_count * piece
    chunk = node_count * piece
    vmem = pl.BlockSpec(memory_space=pltpu.VMEM)
    hbm = pl.BlockSpec(memory_space=pltpu.HBM)
    inputs = (adj, deg, feats, w_self, w_neigh, bias, cot)
    length = node_count // 2
    pairs = col_count // 2
    bf16, f32 = jnp.bfloat16, jnp.float32
    others, peers = col_count - 1, node_count - 1
    sems = pltpu.SemaphoreType.DMA
    return pl.pallas_call(
        functools.partial(layer_kernel, node_count, col_count, piece),
        out_shape=(
            jax.ShapeDtypeStruct((rows, width), bf16),
            jax.ShapeDtypeStruct((rows, width), bf16),
            jax.ShapeDtypeStruct((width, width), f32),
            jax.ShapeDtypeStruct((width, width), f32),
            jax.ShapeDtypeStruct((1, width), f32),
        ),
        in_specs=[hbm] * 7,
        out_specs=(vmem,) * 5,
        scratch_shapes=[
            *[pltpu.VMEM(x.shape, x.dtype) for x in inputs],
            sems((7,)),
            pltpu.VMEM((node_count, width, rows), bf16),
            pltpu.VMEM((width, col_count * rows), f32),
            pltpu.VMEM((rows, width), f32),
            pltpu.VMEM((pairs, width + 16, rows), bf16),
            pltpu.VMEM((pairs, width + 16, rows), bf16),
            pltpu.VMEM((pairs - 1, width + 16, rows), bf16),
            pltpu.VMEM((pairs - 1, width + 16, rows), bf16),
            pltpu.VMEM((col_count * rows, width), bf16),
            pltpu.VMEM((length, rows, width), bf16),
            pltpu.VMEM((length, rows, width), bf16),
            pltpu.VMEM((length, rows, width), bf16),
            pltpu.VMEM((length, rows, width), bf16),
            pltpu.VMEM((col_count, piece + 16, width), bf16),
            pltpu.VMEM((others, piece + 16, width), bf16),
            pltpu.VMEM((node_count, group + 16, width), bf16),
            pltpu.VMEM((peers, group + 16, width), bf16),
            pltpu.VMEM((col_count, chunk, width), bf16),
            sems((node_count,)), sems((node_count,)), sems((node_count,)), sems((node_count,)),
            sems((pairs,)), sems((pairs,)), sems((pairs - 1,)), sems((pairs - 1,)),
            sems((pairs - 1,)), sems((col_count,)), sems((pairs,)),
            sems((length,)), sems((length,)), sems((length,)), sems((length,)),
            sems((others,)), sems((others,)),
            sems((peers,)), sems((peers,)), sems((peers,)), sems((peers,)),
            sems((others,)), sems((others,)),
        ],
        compiler_params=pltpu.CompilerParams(
            collective_id=0, has_side_effects=True, vmem_limit_bytes=63 * 1024 * 1024
        ),
        cost_estimate=pl.CostEstimate(flops=2_500_000_000, bytes_accessed=9_000_000, transcendentals=70_000),
        name="sage_layer",
    )(*inputs)


def finish_kernel(*refs):
    given, results, staged, in_sem, out_sem = refs[:5], refs[5:10], refs[10:15], refs[15], refs[16]
    reads = [pltpu.make_async_copy(given[k], staged[k], in_sem.at[k]) for k in range(5)]
    writes = [pltpu.make_async_copy(staged[k], results[k], out_sem.at[k]) for k in range(5)]
    for read in reads:
        read.start()
    for read, write in zip(reads, writes):
        read.wait()
        write.start()
    for write in writes:
        write.wait()


def finish(results):
    hbm = pl.BlockSpec(memory_space=pltpu.HBM)
    return pl.pallas_call(
        finish_kernel,
        out_shape=tuple(jax.ShapeDtypeStruct(x.shape, x.dtype) for x in results),
        in_specs=[hbm] * 5,
        out_specs=(hbm,) * 5,
        scratch_shapes=[
            *[pltpu.VMEM(x.shape, x.dtype) for x in results],
            pltpu.SemaphoreType.DMA((5,)),
            pltpu.SemaphoreType.DMA((5,)),
        ],
        compiler_params=pltpu.CompilerParams(vmem_limit_bytes=63 * 1024 * 1024),
        name="write_results",
    )(*results)


def shards(node_feats, tile_row, tile_col, tile_bits, w_self, w_neigh, bias, cotangent):
    rows_dev, width_in = node_feats.shape
    node_count = lax.axis_size("nodes")
    col_count = lax.axis_size("cols")
    per_dev = rows_dev // 128
    adj, deg = build(tile_row, tile_col, tile_bits, node_count * per_dev, col_count * per_dev)
    layer_out, feat_grad, self_grad, neigh_grad, bias_grad = finish(
        layer(adj, deg, node_feats, w_self, w_neigh, bias[None, :], cotangent, node_count, col_count)
    )
    return (layer_out, feat_grad, self_grad, neigh_grad, bias_grad[0])


def solution(mesh):
    return jax.shard_map(
        shards,
        mesh=mesh,
        in_specs=(
            P(("nodes", "cols"), None),
            P("nodes", "cols"),
            P("nodes", "cols"),
            P("nodes", "cols", None, None),
            P(),
            P(),
            P(),
            P(("nodes", "cols"), None),
        ),
        out_specs=(P(("nodes", "cols"), None), P(("nodes", "cols"), None), P(), P(), P()),
        check_vma=False,
    )
```
